256 devices in a mesh: batch: 4 (over z_lo), pencil: 64 (over y, x, z_hi, core).
Axes of the slice: x: 4, y: 4, z: 8 (z_hi: 2, z_lo: 4; z = z_hi * 4 + z_lo), core: 2. Of those that a mesh axis runs over, the one named last changes fastest.
Arguments:
- state_field: float32 [8, 128, 32, 32, 128], P('batch', 'pencil'), may hold values from -6 to 6
- spectral_weight: float32 [128, 2, 32, 32, 16], P('pencil'), may hold values from -6 to 6
- local_weight: float32 [32, 32], replicated, may hold values from -1 to 1
- channel_bias: float32 [32], replicated, may hold values from -3 to 3
- cotangent: float32 [8, 128, 32, 32, 128], P('batch', 'pencil'), may hold values from -6 to 6
Outputs:
- layer_out: float32 [8, 128, 32, 32, 128], P('batch', 'pencil')
- grad_state: float32 [8, 128, 32, 32, 128], P('batch', 'pencil')
- grad_spectral: float32 [128, 2, 32, 32, 16], P('pencil')
- grad_local: float32 [32, 32], replicated
- grad_bias: float32 [32], replicated
The draws below stay inside these ranges and needn't reach their ends.
All inputs are finite; a program needn't handle non-finite values.
Results may differ from the reference program's by a relative error of at most 0.00011.
Values sent between devices are 32-bit elements; how exact they have to be, the bound alone decides.
A program may use at most 128 MiB of HBM per device.

```python
import math
import jax
import jax.numpy as jnp
from jax import lax

X = 128
Y = 128
Z = 32
C = 32
MX = 16
MY = 16
MZ = 8
SAMPLES = 8


def levels(stream_key, extent, pieces, smallest, top_value):
    loudness = 1.0
    for dim, shards_of in pieces:
        heights = jax.random.uniform(jax.random.fold_in(jax.random.fold_in(stream_key, 6), dim), (shards_of,), jnp.float32, smallest / len(pieces), top_value / len(pieces))
        loudness = loudness * jnp.repeat(jnp.exp(heights), extent[dim] // shards_of).reshape((-1,) + (1,) * (len(extent) - 1 - dim))
    return loudness


def scatter_about(key, shape, spread, bound, cuts=(), kind=jnp.bfloat16):
    values = jax.random.normal(key, shape, jnp.float32) * spread
    if len(cuts) > 0:
        values = levels(key, shape, cuts, -0.22, 0.18) * values
    return jnp.clip(values, min=-bound, max=bound).astype(kind)


def setup_inputs(seed: int = 0) -> dict:
    seeds = jax.random.split(jax.random.key(seed), 6)
    state_field = scatter_about(seeds[0], (SAMPLES, Y, C, Z, X), 1.0, 6.0, ((0, 4), (1, 64)), jnp.float32)
    spectral_weight = scatter_about(seeds[1], (MX * MZ, 2, C, C, MY), 1.1, 6.0, ((0, 64),), jnp.float32)
    local_weight = scatter_about(seeds[2], (C, C), C ** -0.5, 1.0, (), jnp.float32)
    channel_bias = scatter_about(seeds[3], (C,), 0.5, 3.0, (), jnp.float32)
    cotangent = scatter_about(seeds[4], (SAMPLES, Y, C, Z, X), 1.0, 6.0, ((0, 4), (1, 64)), jnp.float32)
    return {"state_field": state_field, "spectral_weight": spectral_weight, "local_weight": local_weight, "channel_bias": channel_bias, "cotangent": cotangent}


def contract(form, left, right):
    return jnp.einsum(form, left, right, precision=lax.Precision.HIGHEST)

def tables(points, kept_modes):
    position = jnp.arange(points, dtype=jnp.int32)
    mode_order = jnp.arange(kept_modes, dtype=jnp.int32)
    frequency = jnp.where(mode_order < kept_modes // 2, mode_order, points - kept_modes + mode_order)
    phases = position[:, None] * frequency[None, :] % points
    angles = phases.astype(jnp.float32) * (2.0 * math.pi / points)
    return (jnp.cos(angles), jnp.sin(angles))

def spectral_sample(sample, weight):
    cos_x, sin_x = tables(X, MX)
    cos_y, sin_y = tables(Y, MY)
    cos_z, sin_z = tables(Z, MZ)
    scaling = 1.0 / math.sqrt(X * Y * Z)
    x_real = contract('yczx,xk->yczk', sample, cos_x)
    x_imag = -contract('yczx,xk->yczk', sample, sin_x)
    z_real = contract('yczk,zj->kjcy', x_real, cos_z) + contract('yczk,zj->kjcy', x_imag, sin_z)
    z_imag = contract('yczk,zj->kjcy', x_imag, cos_z) - contract('yczk,zj->kjcy', x_real, sin_z)
    z_real = z_real.reshape(MX * MZ, C, Y) * scaling
    z_imag = z_imag.reshape(MX * MZ, C, Y) * scaling
    a_real = contract('mcy,yq->mcq', z_real, cos_y) + contract('mcy,yq->mcq', z_imag, sin_y)
    a_imag = contract('mcy,yq->mcq', z_imag, cos_y) - contract('mcy,yq->mcq', z_real, sin_y)
    w_real = weight[:, 0]
    w_imag = weight[:, 1]
    b_real = contract('miq,mioq->moq', a_real, w_real) - contract('miq,mioq->moq', a_imag, w_imag)
    b_imag = contract('miq,mioq->moq', a_real, w_imag) + contract('miq,mioq->moq', a_imag, w_real)
    y_real = contract('moq,yq->moy', b_real, cos_y) - contract('moq,yq->moy', b_imag, sin_y)
    y_imag = contract('moq,yq->moy', b_imag, cos_y) + contract('moq,yq->moy', b_real, sin_y)
    y_real = y_real.reshape(MX, MZ, C, Y)
    y_imag = y_imag.reshape(MX, MZ, C, Y)
    back_real = contract('kjoy,zj->yozk', y_real, cos_z) - contract('kjoy,zj->yozk', y_imag, sin_z)
    back_imag = contract('kjoy,zj->yozk', y_imag, cos_z) + contract('kjoy,zj->yozk', y_real, sin_z)
    return (contract('yozk,xk->yozx', back_real, cos_x) - contract('yozk,xk->yozx', back_imag, sin_x)) * scaling

def layer(sample, weight, local_weight, channel_bias):
    pre_act = spectral_sample(sample, weight) + contract('yczx,co->yozx', sample, local_weight) + channel_bias[None, :, None, None]
    return jax.nn.gelu(pre_act, approximate=True)

def reference(state_field, spectral_weight, local_weight, channel_bias, cotangent):

    def advance(carry, items):
        sample, grad_out = items
        result, pullback = jax.vjp(layer, sample, spectral_weight, local_weight, channel_bias)
        grad_sample, grad_weight, grad_lw, grad_cb = pullback(grad_out)
        return ((carry[0] + grad_weight, carry[1] + grad_lw, carry[2] + grad_cb), (result, grad_sample))
    start_carry = (jnp.zeros(spectral_weight.shape, jnp.float32), jnp.zeros(local_weight.shape, jnp.float32), jnp.zeros(channel_bias.shape, jnp.float32))
    totals, stacked = lax.scan(advance, start_carry, (state_field, cotangent))
    scaling = 1.0 / math.sqrt(SAMPLES * X * Y * Z)
    return (stacked[0], stacked[1], totals[0], totals[1] * scaling, totals[2] * scaling)
```

```python
import math

import jax
import jax.numpy as jnp
import ml_dtypes
import numpy as np
from jax import lax
from jax.experimental import pallas as pl
from jax.experimental.pallas import tpu as pltpu
from jax.sharding import PartitionSpec as P

X, Y, Z, C = 128, 128, 32, 32
MX, MY, MZ = 16, 16, 8
PEERS, GROUPS = 64, 4
F32, BF16 = jnp.float32, jnp.bfloat16
gelu_scale = math.sqrt(2.0 / math.pi)
cubic_term = 0.044715
MESH = pl.DeviceIdType.MESH


def angles(points, kept_modes):
    order = np.arange(kept_modes)
    frequency = np.where(order < kept_modes // 2, order, points - kept_modes + order)
    phases = (np.arange(points)[:, None] * frequency[None, :]) % points
    theta = phases * (2.0 * np.pi / points)
    return np.cos(theta), np.sin(theta)


def halves(table):
    table = table.astype(np.float32)
    high = table.astype(ml_dtypes.bfloat16)
    low = (table - high.astype(np.float32)).astype(ml_dtypes.bfloat16)
    return high, low


def left(table):
    high, low = halves(table)
    return np.concatenate([high, low, high], axis=1)


def build_tables():
    cos_x, sin_x = angles(X, MX)
    cos_y, sin_y = angles(Y, MY)
    cos_z, sin_z = angles(Z, MZ)
    scaling = 1.0 / math.sqrt(X * Y * Z)
    zf = np.stack([cos_z.T, -sin_z.T], axis=1)
    zf = np.einsum("krz,cd->krcdz", zf, np.eye(8)).reshape(128, 256)
    xf = np.stack(
        [np.stack([cos_x.T, sin_x.T], 1), np.stack([-sin_x.T, cos_x.T], 1)], 1
    )
    xf = np.einsum("kabx,pq->kapqbx", xf, np.eye(2)).reshape(64, 512) * scaling
    cy = cos_y.reshape(64, 2, 16)
    sy = sin_y.reshape(64, 2, 16)
    yf = np.stack([np.stack([cy, sy], 0), np.stack([-sy, cy], 0)], 0)
    yf = np.einsum("abpyq,mn->ymaqpbn", yf, np.eye(2)).reshape(128, 256)
    xi = np.stack(
        [np.stack([cos_x.T, sin_x.T], 1), np.stack([-sin_x.T, cos_x.T], 1)], 0
    )
    xi = np.einsum("akbx,mn->maknbx", xi, np.eye(4)).reshape(128, 1024) * scaling
    xi_high, xi_low = halves(xi)
    return (
        left(zf),
        left(xf),
        left(yf),
        left(yf.T),
        np.concatenate([xi_high, xi_low, xi_high], axis=0),
        left(zf.T),
    )


def split(value):
    high = value.astype(BF16)
    return high, (value - high.astype(F32)).astype(BF16)


def rows_of(value):
    high, low = split(value)
    return jnp.concatenate([high, high, low], axis=0)


def lanes_of(value):
    high, low = split(value)
    return jnp.concatenate([high, high, low], axis=1)


def dot(a, b):
    return jnp.dot(a, b, preferred_element_type=F32)


def dot_nt(a, b):
    return lax.dot_general(a, b, (((1,), (1,)), ((), ())), preferred_element_type=F32)


def dot_tn(a, b):
    return lax.dot_general(a, b, (((0,), (0,)), ((), ())), preferred_element_type=F32)


def iota(shape, dim):
    return lax.broadcasted_iota(jnp.int32, shape, dim)


def roll(value, shift):
    shift = shift % value.shape[1]
    return value if shift == 0 else pltpu.roll(value, shift, 1)


def kernel(
    v_hbm, w_hbm, lw_hbm, bias_ref, cot_hbm,
    zf_hbm, xf_hbm, yf_hbm, yi_hbm, xi_hbm, zi_hbm,
    out_hbm, gstate_hbm, gspec_hbm, glocal_ref, gbias_ref,
    v, w, lw, cot, zf, xf, yf, yi, xi, zi,
    modes, loc, gp, lay, gspec, bw_high, bw_low, kron_f, kron_b,
    flat, spread, s_all, g_all, acc, part, stage1, stage2,
    send0, send1, send2, send3, recv0, recv1, recv2, recv3,
    in_sem, out_sem, send_sem, recv_sem, small_send, small_recv, barrier_dummy,
):
    del barrier_dummy
    me = lax.axis_index("pencil")
    group = lax.axis_index("batch")

    loads = {}

    def load(name, src, dst, slot):
        loads[name] = pltpu.make_async_copy(src, dst, in_sem.at[slot])
        loads[name].start()

    load("zf", zf_hbm, zf, 0)
    for t in range(4):
        load("v%d" % t, v_hbm.at[t], v.at[t], 1 + t)
    load("xf", xf_hbm, xf, 5)
    load("w", w_hbm, w, 6)
    load("yf", yf_hbm, yf, 7)
    load("yi", yi_hbm, yi, 8)
    load("xi", xi_hbm, xi, 9)
    load("zi", zi_hbm, zi, 10)
    load("cot", cot_hbm, cot, 11)
    load("lw", lw_hbm, lw, 12)

    barrier = pltpu.get_barrier_semaphore()

    def greet_pencil(i, carry):
        peer = (me + i) % PEERS
        pl.semaphore_signal(barrier, inc=1, device_id=(group, peer), device_id_type=MESH)
        return carry

    lax.fori_loop(1, PEERS, greet_pencil, 0)
    quad = me // 4 * 4
    for dg in range(1, GROUPS):
        for dj in range(4):
            peer = quad + (me + dj) % 4
            pl.semaphore_signal(
                barrier, inc=1, device_id=((group + dg) % GROUPS, peer), device_id_type=MESH
            )
    greetings = PEERS - 1 + 12

    def z_forward(block2, t, pair):
        res = dot(zf[...], rows_of(block2))
        order = (t % 2) * 2 + t // 2
        for half in range(2):
            row = order * 32 + (2 * pair + half) * 8
            row = row if isinstance(row, int) else pl.multiple_of(row, 8)
            for kz in range(8):
                for ri in range(2):
                    k = kz * 2 + ri
                    modes[kz // 2, pl.ds(row, 8), pl.ds(((kz % 2) * 2 + ri) * 128, 128)] = res[
                        k * 8 : k * 8 + 8, half * 128 : half * 128 + 128
                    ]

    def x_forward(send):
        for kzp in range(4):
            res = dot_nt(xf[...], lanes_of(modes[kzp]))
            for kx in range(16):
                send[kx * 4 + kzp] = res[kx * 4 : kx * 4 + 4]

    def exchange(send, recv, index):
        def body(i, carry):
            peer = (me + i) % PEERS
            pltpu.make_async_remote_copy(
                src_ref=send.at[peer],
                dst_ref=recv.at[me],
                send_sem=send_sem.at[index],
                recv_sem=recv_sem.at[index],
                device_id=(group, peer),
                device_id_type=MESH,
            ).start()
            return carry

        lax.fori_loop(1, PEERS, body, 0)
        recv[me] = send[me]

    def all_here(recv, sem):
        slots = recv.at[pl.ds(0, PEERS - 1)]
        pltpu.make_async_copy(slots, slots, sem).wait()

    lane = iota((16, 128), 1)

    def y_forward(recv):
        got = recv[...].reshape(256, 128)
        res = dot(yf[...], rows_of(got))
        res = res[0:64] + roll(res[64:128], 64)
        rows = []
        for b in range(2):
            total = jnp.zeros((16, 128), F32)
            for g in range(4):
                piece = roll(res[g * 16 : g * 16 + 16], (g - b) * 32)
                total = jnp.where(lane // 32 == g, piece, total)
            rows.append(total)
        return jnp.concatenate(rows, axis=0)

    def y_inverse(value, send):
        tops = []
        for g in range(4):
            first = roll(value[0:16], -g * 32)
            second = roll(value[16:32], (1 - g) * 32)
            tops.append(
                jnp.where(lane < 32, first, jnp.where(lane < 64, second, 0.0))
            )
        top = jnp.concatenate(tops, axis=0)
        both = jnp.concatenate([top, roll(top, 64)], axis=0)
        res = dot(yi[...], rows_of(both))
        send[...] = res.reshape(64, 4, 128)

    row_q = iota((32, 128), 0) % 16

    def masked(value, j):
        high, low = value
        zero = jnp.zeros_like(high)
        picks = [row_q == 2 * j, row_q == 2 * j + 1]

        def pick(part):
            wide = part.astype(F32)
            return jnp.concatenate(
                [jnp.where(p, wide, 0.0).astype(BF16) for p in picks], axis=1
            )

        del zero
        return pick(high), pick(low)

    def x_inverse(recv):
        flat[...] = recv[...].reshape(256, 128)
        for g in range(2):
            pieces = []
            for k4 in range(4):
                kz = g * 4 + k4
                for ri in range(2):
                    start = (kz // 2) * 4 + ri * 2 + kz % 2
                    pieces.append(flat[pl.ds(start, 16, stride=16), :])
            block = jnp.concatenate(pieces, axis=0)
            turned = block.T
            spread[g] = dot(lanes_of(turned), xi[...])

    def z_inverse(t, pair):
        order = (t % 2) * 2 + t // 2
        columns = []
        for half in range(2):
            row = order * 32 + (2 * pair + half) * 8
            row = row if isinstance(row, int) else pl.multiple_of(row, 8)
            tiles = []
            for k in range(16):
                tiles.append(spread[k // 8, pl.ds(row, 8), pl.ds((k % 8) * 128, 128)])
            columns.append(jnp.concatenate(tiles, axis=0))
        block = jnp.concatenate(columns, axis=1)
        return dot(zi[...], rows_of(block))

    def channel_mix(table, src, dst, t, pair):
        cols = []
        for half in range(2):
            zb = 2 * pair + half
            cols.append(src[t, :, pl.ds(zb * 8, 8), :].reshape(256, 128))
        res = dot(table[...], rows_of(jnp.concatenate(cols, axis=1)))
        for half in range(2):
            zb = 2 * pair + half
            dst[t, :, pl.ds(zb * 8, 8), :] = res[:, half * 128 : half * 128 + 128].reshape(
                32, 8, 128
            )

    def pair_of(src, t, pair):
        return jnp.concatenate(
            [
                src[t, pl.ds((2 * pair + half) * 8, 8)].reshape(256, 128)
                for half in range(2)
            ],
            axis=1,
        )

    loads["zf"].wait()
    for t in range(4):
        loads["v%d" % t].wait()
        for pair in range(2):
            z_forward(pair_of(v, t, pair), t, pair)
    loads["xf"].wait()
    x_forward(send0)
    pl.semaphore_wait(barrier, greetings)
    exchange(send0, recv0, 0)

    expand = (iota((256, 32), 0) // 8 == iota((256, 32), 1)).astype(F32).astype(BF16)
    same = iota((256, 256), 0) % 8 == iota((256, 256), 1) % 8
    loads["lw"].wait()
    lw_high, lw_low = split(lw[...])
    for i, part_of in enumerate((lw_high, lw_low, lw_high)):
        once = dot_nt(expand, part_of).astype(BF16)
        kron_f[:, pl.ds(i * 256, 256)] = jnp.where(same, dot_nt(once, expand), 0.0).astype(BF16)
        once = dot(expand, part_of).astype(BF16)
        kron_b[:, pl.ds(i * 256, 256)] = jnp.where(same, dot_nt(once, expand), 0.0).astype(BF16)

    loads["w"].wait()
    zeros = jnp.zeros((32, 32), F32)
    for q in range(16):
        for m in range(2):
            real = w[pl.ds((m * 2 + 0) * 512 + q, 32, stride=16), :]
            imag = w[pl.ds((m * 2 + 1) * 512 + q, 32, stride=16), :]
            for ri, pieces in enumerate(((real, imag), (-imag, real))):
                pieces = list(pieces)
                both = pieces + [zeros, zeros] if m == 0 else [zeros, zeros] + pieces
                high, low = split(jnp.concatenate(both, axis=1))
                row = (m * 2 + ri) * 32
                bw_high[q, pl.ds(row, 32), :] = high
                bw_low[q, pl.ds(row, 32), :] = low

    for t in range(4):
        for pair in range(2):
            channel_mix(kron_f, v, loc, t, pair)

    loads["yf"].wait()
    loads["yi"].wait()
    all_here(recv0, recv_sem.at[0])
    spectrum = y_forward(recv0)
    own = pl.ds(pl.multiple_of(group * 32, 32), 32)
    s_all[own, :] = spectrum

    def share(buffer, index):
        for dg in range(1, GROUPS):
            pltpu.make_async_remote_copy(
                src_ref=buffer.at[own],
                dst_ref=buffer.at[own],
                send_sem=send_sem.at[index],
                recv_sem=recv_sem.at[index],
                device_id=((group + dg) % GROUPS, me),
                device_id_type=MESH,
            ).start()

    parts = split(spectrum)
    mixed = jnp.zeros((32, 128), F32)
    for j in range(8):
        high, low = masked(parts, j)
        right_high = bw_high[2 * j : 2 * j + 2].reshape(256, 128)
        right_low = bw_low[2 * j : 2 * j + 2].reshape(256, 128)
        mixed = mixed + dot(
            jnp.concatenate([high, high, low], axis=1),
            jnp.concatenate([right_high, right_low, right_high], axis=0),
        )
    y_inverse(mixed, send1)
    exchange(send1, recv1, 1)
    share(s_all, 4)

    loads["xi"].wait()
    loads["zi"].wait()
    loads["cot"].wait()
    all_here(recv1, recv_sem.at[1])
    x_inverse(recv1)
    stores = []
    for t in range(4):
        for pair in range(2):
            field = z_inverse(t, pair)
            grads = []
            for half in range(2):
                ob = 2 * pair + half
                pre = field[:, half * 128 : half * 128 + 128].reshape(8, 32, 128)
                pre = pre + loc[t, pl.ds(ob * 8, 8)]
                shift = jnp.concatenate(
                    [jnp.full((1, 32, 128), bias_ref[ob * 8 + o], F32) for o in range(8)], axis=0
                )
                pre = pre + shift
                square = pre * pre
                inner = gelu_scale * (pre + cubic_term * (square * pre))
                bent = jnp.tanh(inner)
                half_up = 0.5 * (1.0 + bent)
                lay[t, pl.ds(ob * 8, 8)] = pre * half_up
                slope = half_up + (0.5 * gelu_scale) * pre * (1.0 - bent * bent) * (
                    1.0 + (3.0 * cubic_term) * square
                )
                grad = cot[t, pl.ds(ob * 8, 8)] * slope
                gp[t, pl.ds(ob * 8, 8)] = grad
                grads.append(grad.reshape(256, 128))
            z_forward(jnp.concatenate(grads, axis=1), t, pair)
        store = pltpu.make_async_copy(lay.at[t], out_hbm.at[t], out_sem.at[t])
        store.start()
        stores.append(store)
    x_forward(send2)
    exchange(send2, recv2, 2)

    acc[...] = jnp.zeros((256, 256), F32)
    for t in range(4):
        for pair in range(2):
            a_cols, b_cols = [], []
            for half in range(2):
                zb = 2 * pair + half
                a_cols.append(v[t, :, pl.ds(zb * 8, 8), :].reshape(256, 128))
                b_cols.append(gp[t, :, pl.ds(zb * 8, 8), :].reshape(256, 128))
            a_high, a_low = split(jnp.concatenate(a_cols, axis=1))
            b_high, b_low = split(jnp.concatenate(b_cols, axis=1))
            acc[...] += dot_nt(
                jnp.concatenate([a_high, a_high, a_low], axis=1),
                jnp.concatenate([b_high, b_low, b_high], axis=1),
            )
    folded = jnp.sum(jnp.where(same, acc[...], 0.0).reshape(32, 8, 256), axis=1)
    pick = (iota((256, 128), 0) // 8 == iota((256, 128), 1)).astype(F32).astype(BF16)
    fold_high, fold_low = split(folded)
    pointwise = dot(
        jnp.concatenate([fold_high, fold_low], axis=1), jnp.concatenate([pick, pick], axis=0)
    )
    dense = pointwise[0:8]
    for k in range(1, 4):
        dense = dense + roll(pointwise[8 * k : 8 * k + 8], 32 * k)
    sums = jnp.sum(gp[0], axis=1)
    for t in range(1, 4):
        sums = sums + jnp.sum(gp[t], axis=1)
    sum_high, sum_low = split(sums)
    ones = jnp.ones((8, 256), BF16)
    bias_row = dot_nt(
        ones,
        jnp.concatenate(
            [
                jnp.concatenate([sum_high, sum_low], axis=1),
                jnp.zeros((96, 256), BF16),
            ],
            axis=0,
        ),
    )
    part[0, 0:8] = dense
    part[0, 8:16] = bias_row
    spot = group * 4 + me % 4
    for dg in range(GROUPS):
        for dj in range(4):
            if dg == 0 and dj == 0:
                continue
            pltpu.make_async_remote_copy(
                src_ref=part.at[0],
                dst_ref=stage1.at[spot],
                send_sem=small_send.at[0],
                recv_sem=small_recv.at[0],
                device_id=((group + dg) % GROUPS, quad + (me + dj) % 4),
                device_id_type=MESH,
            ).start()
    stage1[spot] = part[0]

    for t in range(4):
        for pair in range(2):
            channel_mix(kron_b, gp, loc, t, pair)

    all_here(recv2, recv_sem.at[2])
    grad_modes = y_forward(recv2)
    g_all[own, :] = grad_modes
    parts = split(grad_modes)
    back = jnp.zeros((32, 128), F32)
    for j in range(8):
        high, low = masked(parts, j)
        right_high = jnp.concatenate([bw_high[2 * j], bw_high[2 * j + 1]], axis=1)
        right_low = jnp.concatenate([bw_low[2 * j], bw_low[2 * j + 1]], axis=1)
        back = back + dot_nt(
            jnp.concatenate([high, high, low], axis=1),
            jnp.concatenate([right_high, right_low, right_high], axis=1),
        )
    y_inverse(back, send3)
    exchange(send3, recv3, 3)
    share(g_all, 5)

    pltpu.make_async_copy(
        stage1.at[pl.ds(0, 15)], stage1.at[pl.ds(0, 15)], small_recv.at[0]
    ).wait()
    part[1] = jnp.sum(stage1[...], axis=0)
    for di in range(1, 16):
        pltpu.make_async_remote_copy(
            src_ref=part.at[1],
            dst_ref=stage2.at[me // 4],
            send_sem=small_send.at[1],
            recv_sem=small_recv.at[1],
            device_id=(group, (me + 4 * di) % PEERS),
            device_id_type=MESH,
        ).start()
    stage2[me // 4] = part[1]

    for buffer, index in ((s_all, 4), (g_all, 5)):
        pltpu.make_async_copy(
            buffer.at[pl.ds(0, 96)], buffer.at[pl.ds(0, 96)], recv_sem.at[index]
        ).wait()
    lane8 = iota((8, 128), 1)
    sign = jnp.where(lane8 // 32 % 2 == 0, 1.0, -1.0)
    low_half = lane8 < 64
    for q in range(16):
        s_q = s_all[pl.ds(q, 8, stride=16), :]
        g_q = g_all[pl.ds(q, 8, stride=16), :]
        first = s_q * sign
        second = jnp.where(lane8 // 32 % 2 == 0, roll(s_q, -32), roll(s_q, 32))
        left_rows = jnp.concatenate(
            [
                jnp.where(low_half, first, 0.0),
                jnp.where(low_half, second, 0.0),
                jnp.where(low_half, 0.0, first),
                jnp.where(low_half, 0.0, second),
            ],
            axis=0,
        )
        right_rows = jnp.concatenate([roll(g_q, -32 * g) for g in range(4)], axis=0)
        l_high, l_low = split(left_rows)
        r_high, r_low = split(right_rows)
        res = dot_tn(
            jnp.concatenate([l_high, l_high, l_low], axis=0),
            jnp.concatenate([r_high, r_low, r_high], axis=0),
        )
        gspec[pl.ds(q, 128, stride=16), :] = res[:, 0:32]
    store = pltpu.make_async_copy(gspec, gspec_hbm, out_sem.at[8])
    store.start()
    stores.append(store)

    all_here(recv3, recv_sem.at[3])
    x_inverse(recv3)
    for t in range(4):
        for pair in range(2):
            field = z_inverse(t, pair)
            for half in range(2):
                ob = 2 * pair + half
                loc[t, pl.ds(ob * 8, 8)] += field[:, half * 128 : half * 128 + 128].reshape(
                    8, 32, 128
                )
        store = pltpu.make_async_copy(loc.at[t], gstate_hbm.at[t], out_sem.at[4 + t])
        store.start()
        stores.append(store)

    pltpu.make_async_copy(
        stage2.at[pl.ds(0, 15)], stage2.at[pl.ds(0, 15)], small_recv.at[1]
    ).wait()
    total = jnp.sum(stage2[...], axis=0) * (1.0 / math.sqrt(8 * X * Y * Z))
    for k in range(4):
        glocal_ref[pl.ds(8 * k, 8), :] = roll(total[0:8], -32 * k)[:, 0:32]
    gbias_ref[...] = total[8:9, 0:32]

    for index, buffer in enumerate((send0, send1, send2, send3)):
        all_here(buffer, send_sem.at[index])
    for index, buffer in ((4, s_all), (5, g_all)):
        pltpu.make_async_copy(
            buffer.at[pl.ds(0, 96)], buffer.at[pl.ds(0, 96)], send_sem.at[index]
        ).wait()
    for index, buffer in ((0, stage1), (1, stage2)):
        pltpu.make_async_copy(
            buffer.at[pl.ds(0, 15)], buffer.at[pl.ds(0, 15)], small_send.at[index]
        ).wait()
    for store in stores:
        store.wait()


def hbm(array):
    return pltpu.with_memory_space_constraint(array, pltpu.HBM)


def shards(state_field, spectral_weight, local_weight, channel_bias, cotangent):
    tables = [jnp.asarray(t) for t in build_tables()]
    any_space = pl.BlockSpec(memory_space=pltpu.HBM)
    vmem = pl.BlockSpec(memory_space=pltpu.VMEM)
    smem = pl.BlockSpec(memory_space=pltpu.SMEM)
    cells = (4, 32, 32, 128)
    slots = (64, 4, 128)
    out = pl.pallas_call(
        kernel,
        out_shape=(
            jax.ShapeDtypeStruct(cells, F32),
            jax.ShapeDtypeStruct(cells, F32),
            jax.ShapeDtypeStruct((2048, 32), F32),
            jax.ShapeDtypeStruct((32, 32), F32),
            jax.ShapeDtypeStruct((1, 32), F32),
        ),
        in_specs=[any_space, any_space, any_space, smem, any_space] + [any_space] * 6,
        out_specs=(any_space, any_space, any_space, vmem, vmem),
        scratch_shapes=[
            pltpu.VMEM(cells, F32),
            pltpu.VMEM((2048, 32), F32),
            pltpu.VMEM((32, 32), F32),
            pltpu.VMEM(cells, F32),
            pltpu.VMEM((128, 768), BF16),
            pltpu.VMEM((64, 1536), BF16),
            pltpu.VMEM((128, 768), BF16),
            pltpu.VMEM((256, 384), BF16),
            pltpu.VMEM((384, 1024), BF16),
            pltpu.VMEM((256, 384), BF16),
            pltpu.VMEM((4, 128, 512), F32),
            pltpu.VMEM(cells, F32),
            pltpu.VMEM(cells, F32),
            pltpu.VMEM(cells, F32),
            pltpu.VMEM((2048, 32), F32),
            pltpu.VMEM((16, 128, 128), BF16),
            pltpu.VMEM((16, 128, 128), BF16),
            pltpu.VMEM((256, 768), BF16),
            pltpu.VMEM((256, 768), BF16),
            pltpu.VMEM((256, 128), F32),
            pltpu.VMEM((2, 128, 1024), F32),
            pltpu.VMEM((128, 128), F32),
            pltpu.VMEM((128, 128), F32),
            pltpu.VMEM((256, 256), F32),
            pltpu.VMEM((2, 16, 128), F32),
            pltpu.VMEM((16, 16, 128), F32),
            pltpu.VMEM((16, 16, 128), F32),
        ]
        + [pltpu.VMEM(slots, F32)] * 8
        + [
            pltpu.SemaphoreType.DMA((13,)),
            pltpu.SemaphoreType.DMA((9,)),
            pltpu.SemaphoreType.DMA((6,)),
            pltpu.SemaphoreType.DMA((6,)),
            pltpu.SemaphoreType.DMA((2,)),
            pltpu.SemaphoreType.DMA((2,)),
            pltpu.SMEM((1,), jnp.int32),
        ],
        compiler_params=pltpu.CompilerParams(
            collective_id=0, has_side_effects=True, vmem_limit_bytes=40 * 1024 * 1024
        ),
        name="fno_layer",
    )(
        hbm(state_field.reshape(cells)),
        hbm(jnp.swapaxes(spectral_weight, 3, 4).reshape(2048, 32)),
        hbm(local_weight),
        channel_bias,
        hbm(cotangent.reshape(cells)),
        *[hbm(t) for t in tables],
    )
    layer_out, grad_state, grad_spectral, grad_local, grad_bias = out
    return (
        layer_out.reshape(state_field.shape),
        grad_state.reshape(state_field.shape),
        jnp.swapaxes(grad_spectral.reshape(2, 2, 32, 16, 32), 3, 4),
        grad_local,
        grad_bias.reshape(32),
    )


def solution(mesh):
    cells = P("batch", "pencil", None, None, None)
    modes = P("pencil", None, None, None, None)
    return jax.shard_map(
        shards,
        mesh=mesh,
        in_specs=(cells, modes, P(), P(), cells),
        out_specs=(cells, cells, modes, P(), P()),
        check_vma=False,
    )
```

```python
import math
import types

import jax
import jax.numpy as jnp
import ml_dtypes
import numpy as np
from jax import lax
from jax.experimental import pallas as pl
from jax.experimental.pallas import tpu as pltpu
from jax.sharding import PartitionSpec as P

X, Y, Z, C = 128, 128, 32, 32
MX, MY, MZ = 16, 16, 8
PEERS, GROUPS = 64, 4
F32, BF16 = jnp.float32, jnp.bfloat16
gelu_scale = math.sqrt(2.0 / math.pi)
cubic_term = 0.044715
MESH = pl.DeviceIdType.MESH


def angles(points, kept_modes):
    order = np.arange(kept_modes)
    frequency = np.where(order < kept_modes // 2, order, points - kept_modes + order)
    phases = (np.arange(points)[:, None] * frequency[None, :]) % points
    theta = phases * (2.0 * np.pi / points)
    return np.cos(theta), np.sin(theta)


def halves(table):
    table = table.astype(np.float32)
    high = table.astype(ml_dtypes.bfloat16)
    low = (table - high.astype(np.float32)).astype(ml_dtypes.bfloat16)
    return high, low


def left(table):
    high, low = halves(table)
    return np.concatenate([high, low, high], axis=1)


def build_tables():
    cos_x, sin_x = angles(X, MX)
    cos_y, sin_y = angles(Y, MY)
    cos_z, sin_z = angles(Z, MZ)
    scaling = 1.0 / math.sqrt(X * Y * Z)
    zf = np.stack([cos_z.T, -sin_z.T], axis=1)
    zf = np.einsum("krz,cd->krcdz", zf, np.eye(8)).reshape(128, 256)
    xf = np.stack(
        [np.stack([cos_x.T, sin_x.T], 1), np.stack([-sin_x.T, cos_x.T], 1)], 1
    )
    xf = np.einsum("kabx,pq->kapqbx", xf, np.eye(2)).reshape(64, 512) * scaling
    cy = cos_y.reshape(64, 2, 16)
    sy = sin_y.reshape(64, 2, 16)
    yf = np.stack([np.stack([cy, sy], 0), np.stack([-sy, cy], 0)], 0)
    yf = np.einsum("abpyq,mn->ymaqpbn", yf, np.eye(2)).reshape(128, 256)
    xi = np.stack(
        [np.stack([cos_x.T, sin_x.T], 1), np.stack([-sin_x.T, cos_x.T], 1)], 0
    )
    xi = np.einsum("akbx,mn->maknbx", xi, np.eye(4)).reshape(128, 1024) * scaling
    xi_high, xi_low = halves(xi)
    return (
        left(zf),
        left(xf),
        left(yf),
        left(yf.T),
        np.concatenate([xi_high, xi_low, xi_high], axis=0),
        left(zf.T),
    )


RING = (0, 1, 2, 1)
FAR_FIRST = sorted(
    ((dy, dx) for dy in range(4) for dx in range(4)), key=lambda d: -RING[d[0]] - RING[d[1]]
)


def split(value):
    high = value.astype(BF16)
    return high, (value - high.astype(F32)).astype(BF16)


def rows_of(value):
    high, low = split(value)
    return jnp.concatenate([high, high, low], axis=0)


def lanes_of(value):
    high, low = split(value)
    return jnp.concatenate([high, high, low], axis=1)


def dot(a, b):
    return jnp.dot(a, b, preferred_element_type=F32)


def dot_nt(a, b):
    return lax.dot_general(a, b, (((1,), (1,)), ((), ())), preferred_element_type=F32)


def dot_tn(a, b):
    return lax.dot_general(a, b, (((0,), (0,)), ((), ())), preferred_element_type=F32)


def iota(shape, dim):
    return lax.broadcasted_iota(jnp.int32, shape, dim)


def roll(value, shift):
    shift = shift % value.shape[1]
    return value if shift == 0 else pltpu.roll(value, shift, 1)


def z_forward(r, block2, t, pair):
    res = dot(r.zf[...], rows_of(block2))
    order = (t % 2) * 2 + t // 2
    for half in range(2):
        row = order * 32 + (2 * pair + half) * 8
        for kz in range(8):
            for ri in range(2):
                k = kz * 2 + ri
                r.modes[kz // 2, pl.ds(row, 8), pl.ds(((kz % 2) * 2 + ri) * 128, 128)] = res[
                    k * 8 : k * 8 + 8, half * 128 : half * 128 + 128
                ]


def x_forward(r, send, dispatch):
    for kzp in range(4):
        res = dot_nt(r.xf[...], lanes_of(r.modes[kzp]))
        for kx in range(16):
            send[kx * 4 + kzp] = res[kx * 4 : kx * 4 + 4]
        for dy, dx in FAR_FIRST:
            dispatch(dy, dx, kzp)


def y_forward(r, recv):
    lane = iota((16, 128), 1)
    got = recv[...].reshape(256, 128)
    res = dot(r.yf[...], rows_of(got))
    res = res[0:64] + roll(res[64:128], 64)
    rows = []
    for b in range(2):
        total = jnp.zeros((16, 128), F32)
        for g in range(4):
            piece = roll(res[g * 16 : g * 16 + 16], (g - b) * 32)
            total = jnp.where(lane // 32 == g, piece, total)
        rows.append(total)
    return jnp.concatenate(rows, axis=0)


def y_inverse(r, value, send, my_y, dispatch):
    lane = iota((16, 128), 1)
    tops = []
    for g in range(4):
        first = roll(value[0:16], -g * 32)
        second = roll(value[16:32], (1 - g) * 32)
        tops.append(jnp.where(lane < 32, first, jnp.where(lane < 64, second, 0.0)))
    top = jnp.concatenate(tops, axis=0)
    both = jnp.concatenate([top, roll(top, 64)], axis=0)
    both = rows_of(both)
    for dy in (2, 1, 3, 0):
        to_y = (my_y + dy) % 4
        table = r.yi[pl.ds(pl.multiple_of(to_y * 64, 64), 64), :]
        res = dot(table, both)
        send[pl.ds(to_y * 16, 16)] = res.reshape(16, 4, 128)
        for dx in (2, 1, 3, 0):
            for to_z in range(4):
                dispatch(dy, dx, to_z)


def masked(parts, j):
    row_q = iota((32, 128), 0) % 16
    picks = [row_q == 2 * j, row_q == 2 * j + 1]

    def pick(part):
        wide = part.astype(F32)
        return jnp.concatenate(
            [jnp.where(p, wide, 0.0).astype(BF16) for p in picks], axis=1
        )

    return pick(parts[0]), pick(parts[1])


def x_inverse(r, recv):
    r.flat[...] = recv[...].reshape(256, 128)
    for g in range(2):
        pieces = []
        for k4 in range(4):
            kz = g * 4 + k4
            for ri in range(2):
                start = (kz // 2) * 4 + ri * 2 + kz % 2
                pieces.append(r.flat[pl.ds(start, 16, stride=16), :])
        block = jnp.concatenate(pieces, axis=0)
        turned = block.T
        r.spread[g] = dot(lanes_of(turned), r.xi[...])


def z_inverse(r, t, pair):
    order = (t % 2) * 2 + t // 2
    columns = []
    for half in range(2):
        row = order * 32 + (2 * pair + half) * 8
        tiles = []
        for k in range(16):
            tiles.append(r.spread[k // 8, pl.ds(row, 8), pl.ds((k % 8) * 128, 128)])
        columns.append(jnp.concatenate(tiles, axis=0))
    block = jnp.concatenate(columns, axis=1)
    return dot(r.zi[...], rows_of(block))


def channel_mix(table, src, dst, shift=None):
    for t in range(4):
        for pair in range(2):
            cols = []
            for half in range(2):
                zb = 2 * pair + half
                cols.append(src[t, :, pl.ds(zb * 8, 8), :].reshape(256, 128))
            res = dot(table[...], rows_of(jnp.concatenate(cols, axis=1)))
            for half in range(2):
                zb = 2 * pair + half
                part = res[:, half * 128 : half * 128 + 128].reshape(32, 8, 128)
                if shift is not None:
                    part = part + shift[...]
                dst[t, :, pl.ds(zb * 8, 8), :] = part


def pair_of(src, t, pair):
    return jnp.concatenate(
        [src[t, pl.ds((2 * pair + half) * 8, 8)].reshape(256, 128) for half in range(2)],
        axis=1,
    )


def state_cells(r, t):
    for pair in range(2):
        z_forward(r, pair_of(r.v, t, pair), t, pair)


def same_z():
    return iota((256, 256), 0) % 8 == iota((256, 256), 1) % 8


def pointwise_tables(r):
    expand = (iota((256, 32), 0) // 8 == iota((256, 32), 1)).astype(F32).astype(BF16)
    same = same_z()
    lw_high, lw_low = split(r.lw[...])
    for i, part_of in enumerate((lw_high, lw_low, lw_high)):
        once = dot_nt(expand, part_of).astype(BF16)
        r.kron_f[:, pl.ds(i * 256, 256)] = jnp.where(same, dot_nt(once, expand), 0.0).astype(BF16)
        once = dot(expand, part_of).astype(BF16)
        r.kron_b[:, pl.ds(i * 256, 256)] = jnp.where(same, dot_nt(once, expand), 0.0).astype(BF16)


    for o in range(32):
        r.shift[o] = jnp.full((8, 128), r.bias[o], F32)


def mode_tables(r):
    zeros = jnp.zeros((32, 32), F32)
    for q in range(16):
        rows = []
        for m in range(2):
            real = r.w[pl.ds((m * 2 + 0) * 512 + q, 32, stride=16), :]
            imag = r.w[pl.ds((m * 2 + 1) * 512 + q, 32, stride=16), :]
            for ri, pieces in enumerate(((real, imag), (-imag, real))):
                pieces = list(pieces)
                both = pieces + [zeros, zeros] if m == 0 else [zeros, zeros] + pieces
                rows.append(jnp.concatenate(both, axis=1))
        block = jnp.concatenate(rows, axis=0)
        r.bw_high[q], r.bw_low[q] = split(block)
        r.bwt_high[q], r.bwt_low[q] = split(block.T)


def all_modes(value, right_high, right_low):
    parts = split(value)
    total = jnp.zeros((32, 128), F32)
    for j in range(8):
        high, low = masked(parts, j)
        r_high = right_high[2 * j : 2 * j + 2].reshape(256, 128)
        r_low = right_low[2 * j : 2 * j + 2].reshape(256, 128)
        total = total + dot(
            jnp.concatenate([high, high, low], axis=1),
            jnp.concatenate([r_high, r_low, r_high], axis=0),
        )
    return total


def mix(r, own, my_y, dispatch):
    spectrum = y_forward(r, r.recv0)
    r.s_all[own, :] = spectrum
    mixed = all_modes(spectrum, r.bw_high, r.bw_low)
    y_inverse(r, mixed, r.send1, my_y, dispatch)


def mix_adjoint(r, own, my_y, dispatch, share):
    grad_modes = y_forward(r, r.recv2)
    r.g_all[own, :] = grad_modes
    share()
    back = all_modes(grad_modes, r.bwt_high, r.bwt_low)
    y_inverse(r, back, r.send3, my_y, dispatch)


def cells(r, t):
    for pair in range(2):
        field = z_inverse(r, t, pair)
        columns = []
        for half in range(2):
            pieces = []
            for o8 in range(8):
                o = (2 * pair + half) * 8 + o8
                pre = field[o8 * 32 : o8 * 32 + 32, half * 128 : half * 128 + 128] + r.loc[t, o]
                square = pre * pre
                bent = jnp.tanh(pre * (gelu_scale + (gelu_scale * cubic_term) * square))
                half_up = 0.5 + 0.5 * bent
                r.lay[t, o] = pre * half_up
                rise = (0.5 * gelu_scale) + (1.5 * gelu_scale * cubic_term) * square
                slope = half_up + (pre * rise) * (1.0 - bent * bent)
                grad = r.cot[t, o] * slope
                r.gp[t, o] = grad
                pieces.append(grad)
            columns.append(jnp.concatenate(pieces, axis=0))
        z_forward(r, jnp.concatenate(columns, axis=1), t, pair)


def point_sums(r):
    same = same_z()
    r.acc[...] = jnp.zeros((256, 256), F32)
    for t in range(4):
        for pair in range(2):
            a_cols, b_cols = [], []
            for half in range(2):
                zb = 2 * pair + half
                a_cols.append(r.v[t, :, pl.ds(zb * 8, 8), :].reshape(256, 128))
                b_cols.append(r.gp[t, :, pl.ds(zb * 8, 8), :].reshape(256, 128))
            a_high, a_low = split(jnp.concatenate(a_cols, axis=1))
            b_high, b_low = split(jnp.concatenate(b_cols, axis=1))
            r.acc[...] += dot_nt(
                jnp.concatenate([a_high, a_high, a_low], axis=1),
                jnp.concatenate([b_high, b_low, b_high], axis=1),
            )
    folded = jnp.sum(jnp.where(same, r.acc[...], 0.0).reshape(32, 8, 256), axis=1)
    pick = (iota((256, 128), 0) // 8 == iota((256, 128), 1)).astype(F32).astype(BF16)
    fold_high, fold_low = split(folded)
    pointwise = dot(
        jnp.concatenate([fold_high, fold_low], axis=1), jnp.concatenate([pick, pick], axis=0)
    )
    dense = pointwise[0:8]
    for k in range(1, 4):
        dense = dense + roll(pointwise[8 * k : 8 * k + 8], 32 * k)
    sums = jnp.sum(r.gp[0], axis=1)
    for t in range(1, 4):
        sums = sums + jnp.sum(r.gp[t], axis=1)
    sum_high, sum_low = split(sums)
    ones = jnp.ones((8, 256), BF16)
    bias_row = dot_nt(
        ones,
        jnp.concatenate(
            [jnp.concatenate([sum_high, sum_low], axis=1), jnp.zeros((96, 256), BF16)], axis=0
        ),
    )
    for i in range(8):
        r.part1[i] = dense[i : i + 1]
        r.part1[8 + i] = bias_row[i : i + 1]


def weight_gradient(r):
    lane8 = iota((8, 128), 1)
    sign = jnp.where(lane8 // 32 % 2 == 0, 1.0, -1.0)
    low_half = lane8 < 64
    for q in range(16):
        s_q = r.s_all[pl.ds(q, 8, stride=16), :]
        g_q = r.g_all[pl.ds(q, 8, stride=16), :]
        first = s_q * sign
        second = jnp.where(lane8 // 32 % 2 == 0, roll(s_q, -32), roll(s_q, 32))
        left_rows = jnp.concatenate(
            [
                jnp.where(low_half, first, 0.0),
                jnp.where(low_half, second, 0.0),
                jnp.where(low_half, 0.0, first),
                jnp.where(low_half, 0.0, second),
            ],
            axis=0,
        )
        right_rows = jnp.concatenate([roll(g_q, -32 * g) for g in range(4)], axis=0)
        l_high, l_low = split(left_rows)
        r_high, r_low = split(right_rows)
        res = dot_tn(
            jnp.concatenate([l_high, l_high, l_low], axis=0),
            jnp.concatenate([r_high, r_low, r_high], axis=0),
        )
        r.gspec[pl.ds(q, 128, stride=16), :] = res[:, 0:32]


def final_cells(r, t):
    for pair in range(2):
        field = z_inverse(r, t, pair)
        for half in range(2):
            ob = 2 * pair + half
            r.res[t, pl.ds(ob * 8, 8)] = r.loc[t, pl.ds(ob * 8, 8)] + field[
                :, half * 128 : half * 128 + 128
            ].reshape(8, 32, 128)


CELLS, SLOTS = (4, 32, 32, 128), (64, 4, 128)
IN_NAMES = "v w lw bias cot zf xf yf yi xi zi".split()
OUT_SHAPES = dict(
    lay=(CELLS, F32), loc=(CELLS, F32), gspec=((2048, 32), F32), recv3=(SLOTS, F32),
    total=((16, 1, 128), F32), xi=((384, 1024), BF16), zi=((256, 384), BF16),
)
SCRATCH = dict(
    v=(CELLS, F32), w=((2048, 32), F32), lw=((32, 32), F32), cot=(CELLS, F32),
    zf=((128, 768), BF16), xf=((64, 1536), BF16), yf=((128, 768), BF16), yi=((256, 384), BF16),
    modes=((4, 128, 512), F32), gp=(CELLS, F32),
    bw_high=((16, 128, 128), BF16), bw_low=((16, 128, 128), BF16),
    bwt_high=((16, 128, 128), BF16), bwt_low=((16, 128, 128), BF16),
    kron_f=((256, 768), BF16), kron_b=((256, 768), BF16),
    flat=((256, 128), F32), spread=((2, 128, 1024), F32),
    s_all=((128, 128), F32), g_all=((128, 128), F32), acc=((256, 256), F32),
    part1=((16, 1, 128), F32), stage1=((16, 1, 128), F32),
    part2=((1, 128), F32), stage2=((16, 1, 128), F32), part3=((1, 128), F32),
    shift=((32, 8, 128), F32),
    send0=(SLOTS, F32), send1=(SLOTS, F32), send2=(SLOTS, F32), send3=(SLOTS, F32),
    recv0=(SLOTS, F32), recv1=(SLOTS, F32), recv2=(SLOTS, F32),
)
SEMAPHORES = dict(in_sem=16, send_sem=6, recv_sem=6, small_send=3, small_recv=3)


def kernel(*refs):
    names = [n + "_hbm" for n in IN_NAMES]
    names += list(OUT_SHAPES) + list(SCRATCH) + ["bias"] + list(SEMAPHORES)
    r = types.SimpleNamespace(**dict(zip(names, refs, strict=True)))
    me = lax.axis_index("pencil")
    group = lax.axis_index("batch")
    my_y, my_x, my_z = me // 16, me // 4 % 4, me % 4
    across = (group + 2) % GROUPS

    def peer_of(dy, dx, to_z):
        return (my_y + dy) % 4 * 16 + (my_x + dx) % 4 * 4 + to_z

    barrier = pltpu.get_barrier_semaphore()
    for dy, dx in FAR_FIRST:
        for to_z in range(4):
            pl.semaphore_signal(
                barrier, inc=1, device_id=(across, peer_of(dy, dx, to_z)), device_id_type=MESH
            )
    greetings = PEERS
    around = []
    for dg in range(4):
        for dz in range(4):
            if dg == 0 and dz == 0:
                continue
            near = ((group + dg) % GROUPS, me - my_z + (my_z + dz) % 4)
            around.append(near)
            if dg != 2:
                greetings += 1
                pl.semaphore_signal(barrier, inc=1, device_id=near, device_id_type=MESH)

    loads = {}

    def load(name, src, dst):
        loads[name] = pltpu.make_async_copy(src, dst, r.in_sem.at[len(loads)])
        loads[name].start()

    load("zf", r.zf_hbm, r.zf)
    for t in range(4):
        load("v%d" % t, r.v_hbm.at[t], r.v.at[t])
    for name in "xf bias lw w yf yi xi zi cot".split():
        load(name, getattr(r, name + "_hbm"), getattr(r, name))

    def send_to(send, recv, index):
        def dispatch(dy, dx, to_z):
            peer = peer_of(dy, dx, to_z)
            pltpu.make_async_remote_copy(
                src_ref=send.at[peer],
                dst_ref=recv.at[me],
                send_sem=r.send_sem.at[index],
                recv_sem=r.recv_sem.at[index],
                device_id=(across, peer),
                device_id_type=MESH,
            ).start()

        return dispatch

    def await_bytes(ref, sem):
        pltpu.make_async_copy(ref, ref, sem).wait()

    own = pl.ds(pl.multiple_of(group * 32, 32), 32)

    def share(buffer, index):
        for dg in (2, 1, 3):
            pltpu.make_async_remote_copy(
                src_ref=buffer.at[own],
                dst_ref=buffer.at[own],
                send_sem=r.send_sem.at[index],
                recv_sem=r.recv_sem.at[index],
                device_id=((group + dg) % GROUPS, me),
                device_id_type=MESH,
            ).start()

    spot = group * 4 + my_z
    fifteen = pl.ds(0, 15)

    loads["zf"].wait()
    for t in range(4):
        loads["v%d" % t].wait()
        state_cells(r, t)
    loads["xf"].wait()
    pl.semaphore_wait(barrier, greetings)
    x_forward(r, r.send0, send_to(r.send0, r.recv0, 0))

    loads["lw"].wait()
    loads["bias"].wait()
    pointwise_tables(r)
    loads["w"].wait()
    mode_tables(r)
    channel_mix(r.kron_f, r.v, r.loc, r.shift)

    loads["yf"].wait()
    loads["yi"].wait()
    await_bytes(r.recv0, r.recv_sem.at[0])
    mix(r, own, my_y, send_to(r.send1, r.recv1, 1))

    loads["xi"].wait()
    loads["zi"].wait()
    loads["cot"].wait()
    await_bytes(r.recv1, r.recv_sem.at[1])
    share(r.s_all, 4)
    x_inverse(r, r.recv1)
    for t in range(4):
        cells(r, t)
    x_forward(r, r.send2, send_to(r.send2, r.recv2, 2))

    point_sums(r)
    for i, (to_group, to_peer) in enumerate(around):
        pltpu.make_async_remote_copy(
            src_ref=r.part1.at[to_group * 4 + to_peer % 4],
            dst_ref=r.stage1.at[spot],
            send_sem=r.small_send.at[0],
            recv_sem=r.small_recv.at[0],
            device_id=(to_group, to_peer),
            device_id_type=MESH,
        ).start()
    r.stage1[spot] = r.part1[spot]
    channel_mix(r.kron_b, r.gp, r.loc)

    await_bytes(r.stage1.at[fifteen], r.small_recv.at[0])
    r.part2[...] = jnp.sum(r.stage1[...], axis=0)
    for dy, dx in FAR_FIRST:
        pltpu.make_async_remote_copy(
            src_ref=r.part2,
            dst_ref=r.stage2.at[me // 4],
            send_sem=r.small_send.at[1],
            recv_sem=r.small_recv.at[1],
            device_id=(across, peer_of(dy, dx, my_z)),
            device_id_type=MESH,
        ).start()
    await_bytes(r.recv2, r.recv_sem.at[2])
    mix_adjoint(r, own, my_y, send_to(r.send3, r.recv3, 3), lambda: share(r.g_all, 5))

    await_bytes(r.stage2, r.small_recv.at[1])
    r.part3[...] = jnp.sum(r.stage2[...], axis=0) * (1.0 / math.sqrt(8 * X * Y * Z))
    for to_group, to_peer in around:
        pltpu.make_async_remote_copy(
            src_ref=r.part3,
            dst_ref=r.total.at[across * 4 + my_z],
            send_sem=r.small_send.at[2],
            recv_sem=r.small_recv.at[2],
            device_id=(to_group, to_peer),
            device_id_type=MESH,
        ).start()
    r.total[across * 4 + my_z] = r.part3[...]
    for buffer, index in ((r.s_all, 4), (r.g_all, 5)):
        await_bytes(buffer.at[pl.ds(0, 96)], r.recv_sem.at[index])
    weight_gradient(r)

    for index, buffer in enumerate((r.send0, r.send1, r.send2, r.send3)):
        await_bytes(buffer, r.send_sem.at[index])
    for index, buffer in ((4, r.s_all), (5, r.g_all)):
        await_bytes(buffer.at[pl.ds(0, 96)], r.send_sem.at[index])
    await_bytes(r.stage1.at[fifteen], r.small_send.at[0])
    await_bytes(r.stage2, r.small_send.at[1])
    await_bytes(r.total.at[fifteen], r.small_send.at[2])
    await_bytes(r.total.at[fifteen], r.small_recv.at[2])
    await_bytes(r.recv3, r.recv_sem.at[3])


TAIL_SCRATCH = dict(
    flat=((256, 128), F32), spread=((2, 128, 1024), F32), res=(CELLS, F32),
)


def tail(*refs):
    names = list(OUT_SHAPES) + "layer_out grad_state grad_spectral grad_local grad_bias".split()
    names += list(TAIL_SCRATCH) + ["sem"]
    r = types.SimpleNamespace(**dict(zip(names, refs, strict=True)))
    copies = []

    def copy(src, dst):
        copies.append(pltpu.make_async_copy(src, dst, r.sem.at[len(copies)]))
        copies[-1].start()

    copy(r.lay, r.layer_out)
    copy(r.gspec, r.grad_spectral)
    total = r.total[...].reshape(16, 128)
    for k in range(4):
        r.grad_local[pl.ds(8 * k, 8), :] = roll(total[0:8], -32 * k)[:, 0:32]
    r.grad_bias[...] = total[8:9, 0:32]
    x_inverse(r, r.recv3)
    for t in range(4):
        final_cells(r, t)
        copy(r.res.at[t], r.grad_state.at[t])
    for pending in copies:
        pending.wait()


def vmem(array):
    return pltpu.with_memory_space_constraint(array, pltpu.VMEM)


def hbm(array):
    return pltpu.with_memory_space_constraint(array, pltpu.HBM)


def shards(state_field, spectral_weight, local_weight, channel_bias, cotangent):
    tables = [hbm(jnp.asarray(t)) for t in build_tables()]
    in_hbm = pl.BlockSpec(memory_space=pltpu.HBM)
    in_vmem = pl.BlockSpec(memory_space=pltpu.VMEM)
    held = pl.pallas_call(
        kernel,
        out_shape=tuple(pltpu.VMEM(*s) for s in OUT_SHAPES.values()),
        in_specs=[in_hbm] * len(IN_NAMES),
        out_specs=(in_vmem,) * len(OUT_SHAPES),
        scratch_shapes=[pltpu.VMEM(*s) for s in SCRATCH.values()]
        + [pltpu.SMEM((32,), F32)]
        + [pltpu.SemaphoreType.DMA((n,)) for n in SEMAPHORES.values()],
        compiler_params=pltpu.CompilerParams(
            collective_id=0, has_side_effects=True, vmem_limit_bytes=40 * 1024 * 1024
        ),
        name="fno_layer",
    )(
        hbm(state_field.reshape(CELLS)),
        hbm(jnp.swapaxes(spectral_weight, 3, 4).reshape(2048, 32)),
        hbm(local_weight),
        hbm(channel_bias),
        hbm(cotangent.reshape(CELLS)),
        *tables,
    )
    out = pl.pallas_call(
        tail,
        out_shape=(
            jax.ShapeDtypeStruct(CELLS, F32),
            jax.ShapeDtypeStruct(CELLS, F32),
            jax.ShapeDtypeStruct((2048, 32), F32),
            jax.ShapeDtypeStruct((32, 32), F32),
            jax.ShapeDtypeStruct((1, 32), F32),
        ),
        in_specs=[in_vmem] * len(OUT_SHAPES),
        out_specs=(in_hbm, in_hbm, in_hbm, in_vmem, in_vmem),
        scratch_shapes=[pltpu.VMEM(*s) for s in TAIL_SCRATCH.values()]
        + [pltpu.SemaphoreType.DMA((6,))],
        compiler_params=pltpu.CompilerParams(vmem_limit_bytes=24 * 1024 * 1024),
        name="fno_tail",
    )(*[vmem(h) for h in held])
    layer_out, grad_state, grad_spectral, grad_local, grad_bias = out
    return (
        layer_out.reshape(state_field.shape),
        grad_state.reshape(state_field.shape),
        jnp.swapaxes(grad_spectral.reshape(2, 2, 32, 16, 32), 3, 4),
        grad_local,
        grad_bias.reshape(32),
    )


def solution(mesh):
    cells = P("batch", "pencil", None, None, None)
    modes = P("pencil", None, None, None, None)
    return jax.shard_map(
        shards,
        mesh=mesh,
        in_specs=(cells, modes, P(), P(), cells),
        out_specs=(cells, cells, modes, P(), P()),
        check_vma=False,
    )
```

```python
import math
import types

import jax
import jax.numpy as jnp
import ml_dtypes
import numpy as np
from jax import lax
from jax.experimental import pallas as pl
from jax.experimental.pallas import tpu as pltpu
from jax.sharding import PartitionSpec as P

X, Y, Z, C = 128, 128, 32, 32
MX, MY, MZ = 16, 16, 8
PEERS, GROUPS = 64, 4
F32, BF16 = jnp.float32, jnp.bfloat16
gelu_scale = math.sqrt(2.0 / math.pi)
cubic_term = 0.044715
MESH = pl.DeviceIdType.MESH


def angles(points, kept_modes):
    order = np.arange(kept_modes)
    frequency = np.where(order < kept_modes // 2, order, points - kept_modes + order)
    phases = (np.arange(points)[:, None] * frequency[None, :]) % points
    theta = phases * (2.0 * np.pi / points)
    return np.cos(theta), np.sin(theta)


def halves(table):
    table = table.astype(np.float32)
    high = table.astype(ml_dtypes.bfloat16)
    low = (table - high.astype(np.float32)).astype(ml_dtypes.bfloat16)
    return high, low


def left(table):
    high, low = halves(table)
    return np.concatenate([high, low, high], axis=1)


def build_tables():
    cos_x, sin_x = angles(X, MX)
    cos_y, sin_y = angles(Y, MY)
    cos_z, sin_z = angles(Z, MZ)
    scaling = 1.0 / math.sqrt(X * Y * Z)
    zf = np.stack([cos_z.T, -sin_z.T], axis=1)
    zf = np.einsum("krz,cd->krcdz", zf, np.eye(8)).reshape(128, 256)
    xf = np.stack(
        [np.stack([cos_x.T, sin_x.T], 1), np.stack([-sin_x.T, cos_x.T], 1)], 1
    )
    xf = np.einsum("kabx,pq->kapqbx", xf, np.eye(2)).reshape(64, 512) * scaling
    cy = cos_y.reshape(64, 2, 16)
    sy = sin_y.reshape(64, 2, 16)
    yf = np.stack([np.stack([cy, sy], 0), np.stack([-sy, cy], 0)], 0)
    yf = np.einsum("abpyq,mn->ymaqpbn", yf, np.eye(2)).reshape(128, 256)
    xi = np.stack(
        [np.stack([cos_x.T, sin_x.T], 1), np.stack([-sin_x.T, cos_x.T], 1)], 0
    )
    xi = np.einsum("akbx,mn->maknbx", xi, np.eye(4)).reshape(128, 1024) * scaling
    xi_high, xi_low = halves(xi)
    return (
        left(zf),
        left(xf),
        left(yf),
        left(yf.T.reshape(16, 4, 4, 128).swapaxes(0, 1).reshape(256, 128)),
        np.concatenate([xi_high, xi_low, xi_high], axis=0),
        left(zf.T),
    )


Z_ORDER = (0, 2, 1, 3)
RING = (0, 1, 2, 1)
FAR_FIRST = sorted(
    ((dy, dx) for dy in range(4) for dx in range(4)), key=lambda d: -RING[d[0]] - RING[d[1]]
)


def split(value):
    high = value.astype(BF16)
    return high, (value - high.astype(F32)).astype(BF16)


def rows_of(value):
    high, low = split(value)
    return jnp.concatenate([high, high, low], axis=0)


def lanes_of(value):
    high, low = split(value)
    return jnp.concatenate([high, high, low], axis=1)


def dot(a, b):
    return jnp.dot(a, b, preferred_element_type=F32)


def dot_nt(a, b):
    return lax.dot_general(a, b, (((1,), (1,)), ((), ())), preferred_element_type=F32)


def dot_tn(a, b):
    return lax.dot_general(a, b, (((0,), (0,)), ((), ())), preferred_element_type=F32)


def iota(shape, dim):
    return lax.broadcasted_iota(jnp.int32, shape, dim)


def roll(value, shift):
    shift = shift % value.shape[1]
    return value if shift == 0 else pltpu.roll(value, shift, 1)


def z_forward(r, block2, t, pair):
    res = dot(r.zf[...], rows_of(block2))
    order = (t % 2) * 2 + t // 2
    for half in range(2):
        row = order * 32 + (2 * pair + half) * 8
        for kz in range(8):
            for ri in range(2):
                k = kz * 2 + ri
                r.modes[kz // 2, pl.ds(row, 8), pl.ds(((kz % 2) * 2 + ri) * 128, 128)] = res[
                    k * 8 : k * 8 + 8, half * 128 : half * 128 + 128
                ]


def x_forward(r, send, dispatch):
    for kzp in Z_ORDER:
        res = dot_nt(r.xf[...], lanes_of(r.modes[kzp]))
        send[kzp * 16 : kzp * 16 + 16] = res.reshape(16, 4, 128)
        dispatch(kzp)


def y_forward(r, recv):
    lane = iota((16, 128), 1)
    got = recv[...].reshape(256, 128)
    res = dot(r.yf[...], rows_of(got))
    res = res[0:64] + roll(res[64:128], 64)
    rows = []
    for b in range(2):
        total = jnp.zeros((16, 128), F32)
        for g in range(4):
            piece = roll(res[g * 16 : g * 16 + 16], (g - b) * 32)
            total = jnp.where(lane // 32 == g, piece, total)
        rows.append(total)
    return jnp.concatenate(rows, axis=0)


def y_inverse(r, value, send, dispatch):
    lane = iota((16, 128), 1)
    tops = []
    for g in range(4):
        first = roll(value[0:16], -g * 32)
        second = roll(value[16:32], (1 - g) * 32)
        tops.append(jnp.where(lane < 32, first, jnp.where(lane < 64, second, 0.0)))
    top = jnp.concatenate(tops, axis=0)
    both = jnp.concatenate([top, roll(top, 64)], axis=0)
    both = rows_of(both)
    for to_z in Z_ORDER:
        res = dot(r.yi[to_z * 64 : to_z * 64 + 64, :], both)
        send[to_z * 16 : to_z * 16 + 16] = res.reshape(16, 4, 128)
        dispatch(to_z)


def masked(parts, j):
    row_q = iota((32, 128), 0) % 16
    picks = [row_q == 2 * j, row_q == 2 * j + 1]

    def pick(part):
        wide = part.astype(F32)
        return jnp.concatenate(
            [jnp.where(p, wide, 0.0).astype(BF16) for p in picks], axis=1
        )

    return pick(parts[0]), pick(parts[1])


def x_inverse(r, recv):
    r.flat[...] = recv[...].reshape(256, 128)
    for g in range(2):
        pieces = []
        for k4 in range(4):
            kz = g * 4 + k4
            for ri in range(2):
                start = (kz // 2) * 4 + ri * 2 + kz % 2
                pieces.append(r.flat[pl.ds(start, 16, stride=16), :])
        block = jnp.concatenate(pieces, axis=0)
        turned = block.T
        r.spread[g] = dot(lanes_of(turned), r.xi[...])


def z_inverse(r, t, pair):
    order = (t % 2) * 2 + t // 2
    columns = []
    for half in range(2):
        row = order * 32 + (2 * pair + half) * 8
        tiles = []
        for k in range(16):
            tiles.append(r.spread[k // 8, pl.ds(row, 8), pl.ds((k % 8) * 128, 128)])
        columns.append(jnp.concatenate(tiles, axis=0))
    block = jnp.concatenate(columns, axis=1)
    return dot(r.zi[...], rows_of(block))


def channel_mix(table, src, dst, shift=None):
    for t in range(4):
        for pair in range(2):
            cols = []
            for half in range(2):
                zb = 2 * pair + half
                cols.append(src[t, :, pl.ds(zb * 8, 8), :].reshape(256, 128))
            res = dot(table[...], rows_of(jnp.concatenate(cols, axis=1)))
            for half in range(2):
                zb = 2 * pair + half
                part = res[:, half * 128 : half * 128 + 128].reshape(32, 8, 128)
                if shift is not None:
                    part = part + shift[...]
                dst[t, :, pl.ds(zb * 8, 8), :] = part


def pair_of(src, t, pair):
    return jnp.concatenate(
        [src[t, pl.ds((2 * pair + half) * 8, 8)].reshape(256, 128) for half in range(2)],
        axis=1,
    )


def field_modes(r, field, t):
    for pair in range(2):
        z_forward(r, pair_of(field, t, pair), t, pair)


def same_z():
    return iota((256, 256), 0) % 8 == iota((256, 256), 1) % 8


def pointwise_tables(r):
    expand = (iota((256, 32), 0) // 8 == iota((256, 32), 1)).astype(F32).astype(BF16)
    same = same_z()
    lw_high, lw_low = split(r.lw[...])
    for i, part_of in enumerate((lw_high, lw_low, lw_high)):
        once = dot_nt(expand, part_of).astype(BF16)
        r.kron_f[:, pl.ds(i * 256, 256)] = jnp.where(same, dot_nt(once, expand), 0.0).astype(BF16)
        once = dot(expand, part_of).astype(BF16)
        r.kron_b[:, pl.ds(i * 256, 256)] = jnp.where(same, dot_nt(once, expand), 0.0).astype(BF16)


    for o in range(32):
        r.shift[o] = jnp.full((8, 128), r.bias[o], F32)


def mode_tables(r):
    zeros = jnp.zeros((32, 32), F32)
    for q in range(16):
        rows = []
        for m in range(2):
            real = r.w[pl.ds((m * 2 + 0) * 512 + q, 32, stride=16), :]
            imag = r.w[pl.ds((m * 2 + 1) * 512 + q, 32, stride=16), :]
            for ri, pieces in enumerate(((real, imag), (-imag, real))):
                pieces = list(pieces)
                both = pieces + [zeros, zeros] if m == 0 else [zeros, zeros] + pieces
                rows.append(jnp.concatenate(both, axis=1))
        block = jnp.concatenate(rows, axis=0)
        r.bw_high[q], r.bw_low[q] = split(block)
        r.bwt_high[q], r.bwt_low[q] = split(block.T)


def all_modes(value, right_high, right_low):
    parts = split(value)
    total = jnp.zeros((32, 128), F32)
    for j in range(8):
        high, low = masked(parts, j)
        r_high = right_high[2 * j : 2 * j + 2].reshape(256, 128)
        r_low = right_low[2 * j : 2 * j + 2].reshape(256, 128)
        total = total + dot(
            jnp.concatenate([high, high, low], axis=1),
            jnp.concatenate([r_high, r_low, r_high], axis=0),
        )
    return total


def mix(r, own, dispatch):
    spectrum = y_forward(r, r.recv0)
    r.s_all[own, :] = spectrum
    mixed = all_modes(spectrum, r.bw_high, r.bw_low)
    y_inverse(r, mixed, r.send1, dispatch)


def mix_adjoint(r, own, dispatch):
    grad_modes = y_forward(r, r.recv2)
    r.g_all[own, :] = grad_modes
    back = all_modes(grad_modes, r.bwt_high, r.bwt_low)
    y_inverse(r, back, r.send3, dispatch)


def cells(r, t):
    for pair in range(2):
        field = z_inverse(r, t, pair)
        for half in range(2):
            for o8 in range(8):
                o = (2 * pair + half) * 8 + o8
                pre = field[o8 * 32 : o8 * 32 + 32, half * 128 : half * 128 + 128] + r.loc[t, o]
                square = pre * pre
                bent = jnp.tanh(pre * (gelu_scale + (gelu_scale * cubic_term) * square))
                half_up = 0.5 + 0.5 * bent
                r.lay[t, o] = pre * half_up
                rise = (0.5 * gelu_scale) + (1.5 * gelu_scale * cubic_term) * square
                slope = half_up + (pre * rise) * (1.0 - bent * bent)
                grad = r.cot[t, o] * slope
                r.gp[t, o] = grad


def point_sums(r):
    same = same_z()
    r.acc[...] = jnp.zeros((256, 256), F32)
    for t in range(4):
        for pair in range(2):
            a_cols, b_cols = [], []
            for half in range(2):
                zb = 2 * pair + half
                a_cols.append(r.v[t, :, pl.ds(zb * 8, 8), :].reshape(256, 128))
                b_cols.append(r.gp[t, :, pl.ds(zb * 8, 8), :].reshape(256, 128))
            a_high, a_low = split(jnp.concatenate(a_cols, axis=1))
            b_high, b_low = split(jnp.concatenate(b_cols, axis=1))
            r.acc[...] += dot_nt(
                jnp.concatenate([a_high, a_high, a_low], axis=1),
                jnp.concatenate([b_high, b_low, b_high], axis=1),
            )
    folded = jnp.sum(jnp.where(same, r.acc[...], 0.0).reshape(32, 8, 256), axis=1)
    pick = (iota((256, 128), 0) // 8 == iota((256, 128), 1)).astype(F32).astype(BF16)
    fold_high, fold_low = split(folded)
    pointwise = dot(
        jnp.concatenate([fold_high, fold_low], axis=1), jnp.concatenate([pick, pick], axis=0)
    )
    dense = pointwise[0:8]
    for k in range(1, 4):
        dense = dense + roll(pointwise[8 * k : 8 * k + 8], 32 * k)
    sums = jnp.sum(r.gp[0], axis=1)
    for t in range(1, 4):
        sums = sums + jnp.sum(r.gp[t], axis=1)
    sum_high, sum_low = split(sums)
    ones = jnp.ones((8, 256), BF16)
    bias_row = dot_nt(
        ones,
        jnp.concatenate(
            [jnp.concatenate([sum_high, sum_low], axis=1), jnp.zeros((96, 256), BF16)], axis=0
        ),
    )
    for i in range(8):
        r.part1[i] = dense[i : i + 1]
        r.part1[8 + i] = bias_row[i : i + 1]


def weight_gradient(r):
    lane8 = iota((8, 128), 1)
    sign = jnp.where(lane8 // 32 % 2 == 0, 1.0, -1.0)
    low_half = lane8 < 64
    for q in range(16):
        s_q = r.s_all[pl.ds(q, 8, stride=16), :]
        g_q = r.g_all[pl.ds(q, 8, stride=16), :]
        first = s_q * sign
        second = jnp.where(lane8 // 32 % 2 == 0, roll(s_q, -32), roll(s_q, 32))
        left_rows = jnp.concatenate(
            [
                jnp.where(low_half, first, 0.0),
                jnp.where(low_half, second, 0.0),
                jnp.where(low_half, 0.0, first),
                jnp.where(low_half, 0.0, second),
            ],
            axis=0,
        )
        right_rows = jnp.concatenate([roll(g_q, -32 * g) for g in range(4)], axis=0)
        l_high, l_low = split(left_rows)
        r_high, r_low = split(right_rows)
        res = dot_tn(
            jnp.concatenate([l_high, l_high, l_low], axis=0),
            jnp.concatenate([r_high, r_low, r_high], axis=0),
        )
        r.gspec[pl.ds(q, 128, stride=16), :] = res[:, 0:32]


def final_cells(r, t):
    for pair in range(2):
        field = z_inverse(r, t, pair)
        for half in range(2):
            ob = 2 * pair + half
            r.res[t, pl.ds(ob * 8, 8)] = r.loc[t, pl.ds(ob * 8, 8)] + field[
                :, half * 128 : half * 128 + 128
            ].reshape(8, 32, 128)


CELLS, SLOTS = (4, 32, 32, 128), (64, 4, 128)
IN_NAMES = ["v", "w", "lw", "bias", "cot", "zf", "xf", "yf", "yi", "xi", "zi"]
OUT_SHAPES = dict(
    lay=(CELLS, F32), loc=(CELLS, F32), gspec=((2048, 32), F32), recv3=(SLOTS, F32),
    total=((16, 1, 128), F32), xi=((384, 1024), BF16), zi=((256, 384), BF16),
)
SCRATCH = dict(
    v=(CELLS, F32), w=((2048, 32), F32), lw=((32, 32), F32), cot=(CELLS, F32),
    zf=((128, 768), BF16), xf=((64, 1536), BF16), yf=((128, 768), BF16), yi=((256, 384), BF16),
    modes=((4, 128, 512), F32), gp=(CELLS, F32),
    bw_high=((16, 128, 128), BF16), bw_low=((16, 128, 128), BF16),
    bwt_high=((16, 128, 128), BF16), bwt_low=((16, 128, 128), BF16),
    kron_f=((256, 768), BF16), kron_b=((256, 768), BF16),
    flat=((256, 128), F32), spread=((2, 128, 1024), F32),
    s_all=((128, 128), F32), g_all=((128, 128), F32), acc=((256, 256), F32),
    part1=((16, 1, 128), F32), stage1=((16, 1, 128), F32),
    part2=((1, 128), F32), stage2=((16, 1, 128), F32), part3=((1, 128), F32),
    shift=((32, 8, 128), F32),
    send0=(SLOTS, F32), send1=(SLOTS, F32), send2=(SLOTS, F32), send3=(SLOTS, F32),
    recv0=(SLOTS, F32), recv1=(SLOTS, F32), recv2=(SLOTS, F32),
)
SEMAPHORES = dict(in_sem=16, send_sem=6, recv_sem=6, small_send=3, small_recv=3)


def kernel(*refs):
    names = [n + "_hbm" for n in IN_NAMES]
    names += list(OUT_SHAPES) + list(SCRATCH) + ["bias"] + list(SEMAPHORES)
    r = types.SimpleNamespace(**dict(zip(names, refs, strict=True)))
    me = lax.axis_index("pencil")
    group = lax.axis_index("batch")
    my_y, my_x, my_z = me // 16, me // 4 % 4, me % 4
    across = (group + 2) % GROUPS

    def peer_of(dy, dx, to_z):
        return (my_y + dy) % 4 * 16 + (my_x + dx) % 4 * 4 + to_z

    barrier = pltpu.get_barrier_semaphore()
    for dy, dx in FAR_FIRST:
        for to_z in range(4):
            pl.semaphore_signal(
                barrier, inc=1, device_id=(across, peer_of(dy, dx, to_z)), device_id_type=MESH
            )
    greetings = PEERS
    around = []
    for dg in range(4):
        for dz in range(4):
            if dg == 0 and dz == 0:
                continue
            near = ((group + dg) % GROUPS, me - my_z + (my_z + dz) % 4)
            around.append(near)
            if dg != 2:
                greetings += 1
                pl.semaphore_signal(barrier, inc=1, device_id=near, device_id_type=MESH)

    for dy, dx in FAR_FIRST[:-1]:
        greetings += 1
        pl.semaphore_signal(
            barrier, inc=1, device_id=(group, peer_of(dy, dx, my_z)), device_id_type=MESH
        )

    loads = {}

    def load(name, src, dst):
        loads[name] = pltpu.make_async_copy(src, dst, r.in_sem.at[len(loads)])
        loads[name].start()

    load("zf", r.zf_hbm, r.zf)
    for t in range(4):
        load("v%d" % t, r.v_hbm.at[t], r.v.at[t])
    for name in ("xf", "bias", "lw", "w", "yf", "yi", "xi", "zi", "cot"):
        load(name, getattr(r, name + "_hbm"), getattr(r, name))

    def send_to(send, recv, index):
        def dispatch(to_z):
            for dy, dx in FAR_FIRST:
                peer = peer_of(dy, dx, to_z)
                pltpu.make_async_remote_copy(
                    src_ref=send.at[to_z * 16 + peer // 4],
                    dst_ref=recv.at[me],
                    send_sem=r.send_sem.at[index],
                    recv_sem=r.recv_sem.at[index],
                    device_id=(across, peer),
                    device_id_type=MESH,
                ).start()

        return dispatch

    def await_bytes(ref, sem):
        pltpu.make_async_copy(ref, ref, sem).wait()

    own = pl.ds(pl.multiple_of(group * 32, 32), 32)

    def share(buffer, index):
        for dg in (2, 1, 3):
            pltpu.make_async_remote_copy(
                src_ref=buffer.at[own],
                dst_ref=buffer.at[own],
                send_sem=r.send_sem.at[index],
                recv_sem=r.recv_sem.at[index],
                device_id=((group + dg) % GROUPS, me),
                device_id_type=MESH,
            ).start()

    spot = group * 4 + my_z
    fifteen = pl.ds(0, 15)

    loads["zf"].wait()
    for t in range(4):
        loads["v%d" % t].wait()
        field_modes(r, r.v, t)
    loads["xf"].wait()
    x_forward(r, r.send0, lambda to_z: None)
    pl.semaphore_wait(barrier, greetings)
    for to_z in Z_ORDER:
        send_to(r.send0, r.recv0, 0)(to_z)

    loads["lw"].wait()
    loads["bias"].wait()
    pointwise_tables(r)
    loads["w"].wait()
    mode_tables(r)
    channel_mix(r.kron_f, r.v, r.loc, r.shift)

    loads["yf"].wait()
    loads["yi"].wait()
    await_bytes(r.recv0, r.recv_sem.at[0])
    mix(r, own, send_to(r.send1, r.recv1, 1))

    loads["xi"].wait()
    loads["zi"].wait()
    loads["cot"].wait()
    await_bytes(r.recv1, r.recv_sem.at[1])
    share(r.s_all, 4)
    x_inverse(r, r.recv1)
    for t in range(4):
        cells(r, t)
    for t in range(4):
        field_modes(r, r.gp, t)
    x_forward(r, r.send2, send_to(r.send2, r.recv2, 2))

    point_sums(r)
    for i, (to_group, to_peer) in enumerate(around):
        pltpu.make_async_remote_copy(
            src_ref=r.part1.at[to_group * 4 + to_peer % 4],
            dst_ref=r.stage1.at[spot],
            send_sem=r.small_send.at[0],
            recv_sem=r.small_recv.at[0],
            device_id=(to_group, to_peer),
            device_id_type=MESH,
        ).start()
    r.stage1[spot] = r.part1[spot]
    channel_mix(r.kron_b, r.gp, r.loc)

    await_bytes(r.stage1.at[fifteen], r.small_recv.at[0])
    r.part2[...] = jnp.sum(r.stage1[...], axis=0)
    for dy, dx in FAR_FIRST[:-1]:
        pltpu.make_async_remote_copy(
            src_ref=r.part2,
            dst_ref=r.stage2.at[me // 4],
            send_sem=r.small_send.at[1],
            recv_sem=r.small_recv.at[1],
            device_id=(group, peer_of(dy, dx, my_z)),
            device_id_type=MESH,
        ).start()
    r.stage2[me // 4] = r.part2[...]
    await_bytes(r.recv2, r.recv_sem.at[2])
    mix_adjoint(r, own, send_to(r.send3, r.recv3, 3))
    share(r.g_all, 5)

    await_bytes(r.stage2.at[fifteen], r.small_recv.at[1])
    r.part3[...] = jnp.sum(r.stage2[...], axis=0) * (1.0 / math.sqrt(8 * X * Y * Z))
    for to_group, to_peer in around:
        pltpu.make_async_remote_copy(
            src_ref=r.part3,
            dst_ref=r.total.at[spot],
            send_sem=r.small_send.at[2],
            recv_sem=r.small_recv.at[2],
            device_id=(to_group, to_peer),
            device_id_type=MESH,
        ).start()
    r.total[spot] = r.part3[...]
    for buffer, index in ((r.s_all, 4), (r.g_all, 5)):
        await_bytes(buffer.at[pl.ds(0, 96)], r.recv_sem.at[index])
    weight_gradient(r)

    for index, buffer in enumerate((r.send0, r.send1, r.send2, r.send3)):
        await_bytes(buffer, r.send_sem.at[index])
    for index, buffer in ((4, r.s_all), (5, r.g_all)):
        await_bytes(buffer.at[pl.ds(0, 96)], r.send_sem.at[index])
    await_bytes(r.stage1.at[fifteen], r.small_send.at[0])
    await_bytes(r.stage2.at[fifteen], r.small_send.at[1])
    await_bytes(r.total.at[fifteen], r.small_send.at[2])
    await_bytes(r.total.at[fifteen], r.small_recv.at[2])
    await_bytes(r.recv3, r.recv_sem.at[3])


TAIL_SCRATCH = dict(
    flat=((256, 128), F32), spread=((2, 128, 1024), F32), res=(CELLS, F32),
)


def tail(*refs):
    names = list(OUT_SHAPES) + ["layer_out", "grad_state", "grad_spectral", "grad_local", "grad_bias"]
    names += list(TAIL_SCRATCH) + ["sem"]
    r = types.SimpleNamespace(**dict(zip(names, refs, strict=True)))
    copies = []

    def copy(src, dst):
        copies.append(pltpu.make_async_copy(src, dst, r.sem.at[len(copies)]))
        copies[-1].start()

    copy(r.lay, r.layer_out)
    copy(r.gspec, r.grad_spectral)
    total = r.total[...].reshape(16, 128)
    for k in range(4):
        r.grad_local[pl.ds(8 * k, 8), :] = roll(total[0:8], -32 * k)[:, 0:32]
    r.grad_bias[...] = total[8:9, 0:32]
    x_inverse(r, r.recv3)
    for t in range(4):
        final_cells(r, t)
        copy(r.res.at[t], r.grad_state.at[t])
    for pending in copies:
        pending.wait()


def vmem(array):
    return pltpu.with_memory_space_constraint(array, pltpu.VMEM)


def hbm(array):
    return pltpu.with_memory_space_constraint(array, pltpu.HBM)


def shards(state_field, spectral_weight, local_weight, channel_bias, cotangent):
    tables = [hbm(jnp.asarray(t)) for t in build_tables()]
    in_hbm = pl.BlockSpec(memory_space=pltpu.HBM)
    in_vmem = pl.BlockSpec(memory_space=pltpu.VMEM)
    held = pl.pallas_call(
        kernel,
        out_shape=tuple(pltpu.VMEM(*s) for s in OUT_SHAPES.values()),
        in_specs=[in_hbm] * len(IN_NAMES),
        out_specs=(in_vmem,) * len(OUT_SHAPES),
        scratch_shapes=[pltpu.VMEM(*s) for s in SCRATCH.values()]
        + [pltpu.SMEM((32,), F32)]
        + [pltpu.SemaphoreType.DMA((n,)) for n in SEMAPHORES.values()],
        compiler_params=pltpu.CompilerParams(
            collective_id=0, has_side_effects=True, vmem_limit_bytes=40 * 1024 * 1024
        ),
        name="fno_layer",
    )(
        hbm(state_field.reshape(CELLS)),
        hbm(jnp.swapaxes(spectral_weight, 3, 4).reshape(2048, 32)),
        hbm(local_weight),
        hbm(channel_bias),
        hbm(cotangent.reshape(CELLS)),
        *tables,
    )
    out = pl.pallas_call(
        tail,
        out_shape=(
            jax.ShapeDtypeStruct(CELLS, F32),
            jax.ShapeDtypeStruct(CELLS, F32),
            jax.ShapeDtypeStruct((2048, 32), F32),
            jax.ShapeDtypeStruct((32, 32), F32),
            jax.ShapeDtypeStruct((1, 32), F32),
        ),
        in_specs=[in_vmem] * len(OUT_SHAPES),
        out_specs=(in_hbm, in_hbm, in_hbm, in_vmem, in_vmem),
        scratch_shapes=[pltpu.VMEM(*s) for s in TAIL_SCRATCH.values()]
        + [pltpu.SemaphoreType.DMA((6,))],
        compiler_params=pltpu.CompilerParams(vmem_limit_bytes=24 * 1024 * 1024),
        name="fno_tail",
    )(*[vmem(h) for h in held])
    layer_out, grad_state, grad_spectral, grad_local, grad_bias = out
    return (
        layer_out.reshape(state_field.shape),
        grad_state.reshape(state_field.shape),
        jnp.swapaxes(grad_spectral.reshape(2, 2, 32, 16, 32), 3, 4),
        grad_local,
        grad_bias.reshape(32),
    )


def solution(mesh):
    cells = P("batch", "pencil", None, None, None)
    modes = P("pencil", None, None, None, None)
    return jax.shard_map(
        shards,
        mesh=mesh,
        in_specs=(cells, modes, P(), P(), cells),
        out_specs=(cells, cells, modes, P(), P()),
        check_vma=False,
    )
```

```python
import math
import types

import jax
import jax.numpy as jnp
import ml_dtypes
import numpy as np
from jax import lax
from jax.experimental import pallas as pl
from jax.experimental.pallas import tpu as pltpu
from jax.sharding import PartitionSpec as P

X, Y, Z, C = 128, 128, 32, 32
MX, MY, MZ = 16, 16, 8
PEERS, GROUPS = 64, 4
F32, BF16 = jnp.float32, jnp.bfloat16
gelu_scale = math.sqrt(2.0 / math.pi)
cubic_term = 0.044715
MESH = pl.DeviceIdType.MESH


def angles(points, kept_modes):
    order = np.arange(kept_modes)
    frequency = np.where(order < kept_modes // 2, order, points - kept_modes + order)
    phases = (np.arange(points)[:, None] * frequency[None, :]) % points
    theta = phases * (2.0 * np.pi / points)
    return np.cos(theta), np.sin(theta)


def halves(table):
    table = table.astype(np.float32)
    high = table.astype(ml_dtypes.bfloat16)
    low = (table - high.astype(np.float32)).astype(ml_dtypes.bfloat16)
    return high, low


def left(table):
    high, low = halves(table)
    return np.concatenate([high, low, high], axis=1)


def build_tables():
    cos_x, sin_x = angles(X, MX)
    cos_y, sin_y = angles(Y, MY)
    cos_z, sin_z = angles(Z, MZ)
    scaling = 1.0 / math.sqrt(X * Y * Z)
    zf = np.stack([cos_z.T, -sin_z.T], axis=1)
    zf = np.einsum("krz,cd->krcdz", zf, np.eye(8)).reshape(128, 256)
    xf = np.stack(
        [np.stack([cos_x.T, sin_x.T], 1), np.stack([-sin_x.T, cos_x.T], 1)], 1
    )
    xf = np.einsum("kabx,pq->kapqbx", xf, np.eye(2)).reshape(64, 512) * scaling
    cy = cos_y.reshape(64, 2, 16)
    sy = sin_y.reshape(64, 2, 16)
    yf = np.stack([np.stack([cy, sy], 0), np.stack([-sy, cy], 0)], 0)
    yf = np.einsum("abpyq,mn->ymaqpbn", yf, np.eye(2)).reshape(128, 256)
    xi = np.stack(
        [np.stack([cos_x.T, sin_x.T], 1), np.stack([-sin_x.T, cos_x.T], 1)], 0
    )
    xi = np.einsum("akbx,mn->maknbx", xi, np.eye(4)).reshape(128, 1024) * scaling
    xi_high, xi_low = halves(xi)
    return (
        left(zf),
        left(xf),
        left(yf),
        left(yf.T.reshape(16, 4, 4, 128).swapaxes(0, 1).reshape(256, 128)),
        np.concatenate([xi_high, xi_low, xi_high], axis=0),
        left(zf.T),
    )


Z_ORDER = (0, 2, 1, 3)
RING = (0, 1, 2, 1)
FAR_FIRST = sorted(
    ((dy, dx) for dy in range(4) for dx in range(4)), key=lambda d: -RING[d[0]] - RING[d[1]]
)


def split(value):
    high = value.astype(BF16)
    return high, (value - high.astype(F32)).astype(BF16)


def rows_of(value):
    high, low = split(value)
    return jnp.concatenate([high, high, low], axis=0)


def lanes_of(value):
    high, low = split(value)
    return jnp.concatenate([high, high, low], axis=1)


def dot(a, b):
    return jnp.dot(a, b, preferred_element_type=F32)


def dot_nt(a, b):
    return lax.dot_general(a, b, (((1,), (1,)), ((), ())), preferred_element_type=F32)


def dot_tn(a, b):
    return lax.dot_general(a, b, (((0,), (0,)), ((), ())), preferred_element_type=F32)


def iota(shape, dim):
    return lax.broadcasted_iota(jnp.int32, shape, dim)


def roll(value, shift):
    shift = shift % value.shape[1]
    return value if shift == 0 else pltpu.roll(value, shift, 1)


def z_forward(r, block2, t, pair):
    res = dot(r.zf[...], rows_of(block2))
    order = (t % 2) * 2 + t // 2
    for half in range(2):
        row = order * 32 + (2 * pair + half) * 8
        for kz in range(8):
            for ri in range(2):
                k = kz * 2 + ri
                r.modes[kz // 2, pl.ds(row, 8), pl.ds(((kz % 2) * 2 + ri) * 128, 128)] = res[
                    k * 8 : k * 8 + 8, half * 128 : half * 128 + 128
                ]


def x_forward(r, send, dispatch):
    for kzp in Z_ORDER:
        res = dot_nt(r.xf[...], lanes_of(r.modes[kzp]))
        send[kzp * 16 : kzp * 16 + 16] = res.reshape(16, 4, 128)
        dispatch(kzp)


def y_forward(r, recv):
    lane = iota((16, 128), 1)
    got = recv[...].reshape(256, 128)
    res = dot(r.yf[...], rows_of(got))
    res = res[0:64] + roll(res[64:128], 64)
    rows = []
    for b in range(2):
        total = jnp.zeros((16, 128), F32)
        for g in range(4):
            piece = roll(res[g * 16 : g * 16 + 16], (g - b) * 32)
            total = jnp.where(lane // 32 == g, piece, total)
        rows.append(total)
    return jnp.concatenate(rows, axis=0)


def y_inverse(r, value, send, dispatch):
    lane = iota((16, 128), 1)
    tops = []
    for g in range(4):
        first = roll(value[0:16], -g * 32)
        second = roll(value[16:32], (1 - g) * 32)
        tops.append(jnp.where(lane < 32, first, jnp.where(lane < 64, second, 0.0)))
    top = jnp.concatenate(tops, axis=0)
    both = jnp.concatenate([top, roll(top, 64)], axis=0)
    both = rows_of(both)
    for to_z in Z_ORDER:
        res = dot(r.yi[to_z * 64 : to_z * 64 + 64, :], both)
        send[to_z * 16 : to_z * 16 + 16] = res.reshape(16, 4, 128)
        dispatch(to_z)


def masked(parts, j):
    row_q = iota((32, 128), 0) % 16
    picks = [row_q == 2 * j, row_q == 2 * j + 1]

    def pick(part):
        wide = part.astype(F32)
        return jnp.concatenate(
            [jnp.where(p, wide, 0.0).astype(BF16) for p in picks], axis=1
        )

    return pick(parts[0]), pick(parts[1])


def x_inverse(r, recv):
    r.flat[...] = recv[...].reshape(256, 128)
    for g in range(2):
        pieces = []
        for k4 in range(4):
            kz = g * 4 + k4
            for ri in range(2):
                start = (kz // 2) * 4 + ri * 2 + kz % 2
                pieces.append(r.flat[pl.ds(start, 16, stride=16), :])
        block = jnp.concatenate(pieces, axis=0)
        turned = block.T
        r.spread[g] = dot(lanes_of(turned), r.xi[...])


def z_inverse(r, t, pair):
    order = (t % 2) * 2 + t // 2
    columns = []
    for half in range(2):
        row = order * 32 + (2 * pair + half) * 8
        tiles = []
        for k in range(16):
            tiles.append(r.spread[k // 8, pl.ds(row, 8), pl.ds((k % 8) * 128, 128)])
        columns.append(jnp.concatenate(tiles, axis=0))
    block = jnp.concatenate(columns, axis=1)
    return dot(r.zi[...], rows_of(block))


def channel_mix(table, src, dst, shift=None):
    for t in range(4):
        for pair in range(2):
            cols = []
            for half in range(2):
                zb = 2 * pair + half
                cols.append(src[t, :, pl.ds(zb * 8, 8), :].reshape(256, 128))
            res = dot(table[...], rows_of(jnp.concatenate(cols, axis=1)))
            for half in range(2):
                zb = 2 * pair + half
                part = res[:, half * 128 : half * 128 + 128].reshape(32, 8, 128)
                if shift is not None:
                    part = part + shift[...]
                dst[t, :, pl.ds(zb * 8, 8), :] = part


def pair_of(src, t, pair):
    return jnp.concatenate(
        [src[t, pl.ds((2 * pair + half) * 8, 8)].reshape(256, 128) for half in range(2)],
        axis=1,
    )


def field_modes(r, field, t):
    for pair in range(2):
        z_forward(r, pair_of(field, t, pair), t, pair)


def same_z():
    return iota((256, 256), 0) % 8 == iota((256, 256), 1) % 8


def pointwise_tables(r):
    expand = (iota((256, 32), 0) // 8 == iota((256, 32), 1)).astype(F32).astype(BF16)
    same = same_z()
    lw_high, lw_low = split(r.lw[...])
    for i, part_of in enumerate((lw_high, lw_low, lw_high)):
        once = dot_nt(expand, part_of).astype(BF16)
        r.kron_f[:, pl.ds(i * 256, 256)] = jnp.where(same, dot_nt(once, expand), 0.0).astype(BF16)
        once = dot(expand, part_of).astype(BF16)
        r.kron_b[:, pl.ds(i * 256, 256)] = jnp.where(same, dot_nt(once, expand), 0.0).astype(BF16)


    for o in range(32):
        r.shift[o] = jnp.full((8, 128), r.bias[o], F32)


def mode_tables(r):
    zeros = jnp.zeros((32, 32), F32)
    for q in range(16):
        rows = []
        for m in range(2):
            real = r.w[pl.ds((m * 2 + 0) * 512 + q, 32, stride=16), :]
            imag = r.w[pl.ds((m * 2 + 1) * 512 + q, 32, stride=16), :]
            for ri, pieces in enumerate(((real, imag), (-imag, real))):
                pieces = list(pieces)
                both = pieces + [zeros, zeros] if m == 0 else [zeros, zeros] + pieces
                rows.append(jnp.concatenate(both, axis=1))
        block = jnp.concatenate(rows, axis=0)
        r.bw_high[q], r.bw_low[q] = split(block)
        r.bwt_high[q], r.bwt_low[q] = split(block.T)


def all_modes(value, right_high, right_low):
    parts = split(value)
    lefts = [masked(parts, j) for j in range(8)]
    high = jnp.concatenate([l[0] for l in lefts], axis=1)
    low = jnp.concatenate([l[1] for l in lefts], axis=1)
    r_high = right_high[...].reshape(2048, 128)
    r_low = right_low[...].reshape(2048, 128)
    both = dot(jnp.concatenate([high, low], axis=0), r_high)
    return both[0:32] + both[32:64] + dot(high, r_low)


def mix(r, own, dispatch):
    spectrum = y_forward(r, r.recv0)
    r.s_all[own, :] = spectrum
    mixed = all_modes(spectrum, r.bw_high, r.bw_low)
    y_inverse(r, mixed, r.send1, dispatch)


def mix_adjoint(r, own, dispatch, share):
    grad_modes = y_forward(r, r.recv2)
    r.g_all[own, :] = grad_modes
    share()
    back = all_modes(grad_modes, r.bwt_high, r.bwt_low)
    y_inverse(r, back, r.send3, dispatch)


def cells(r, t):
    for pair in range(2):
        field = z_inverse(r, t, pair)
        for half in range(2):
            for o8 in range(8):
                o = (2 * pair + half) * 8 + o8
                pre = field[o8 * 32 : o8 * 32 + 32, half * 128 : half * 128 + 128] + r.loc[t, o]
                square = pre * pre
                bent = jnp.tanh(pre * (gelu_scale + (gelu_scale * cubic_term) * square))
                half_up = 0.5 + 0.5 * bent
                r.lay[t, o] = pre * half_up
                rise = (0.5 * gelu_scale) + (1.5 * gelu_scale * cubic_term) * square
                slope = half_up + (pre * rise) * (1.0 - bent * bent)
                grad = r.cot[t, o] * slope
                r.gp[t, o] = grad


def point_sums(r):
    same = same_z()
    r.acc[...] = jnp.zeros((256, 256), F32)
    for t in range(4):
        for pair in range(2):
            a_cols, b_cols = [], []
            for half in range(2):
                zb = 2 * pair + half
                a_cols.append(r.v[t, :, pl.ds(zb * 8, 8), :].reshape(256, 128))
                b_cols.append(r.gp[t, :, pl.ds(zb * 8, 8), :].reshape(256, 128))
            a_high, a_low = split(jnp.concatenate(a_cols, axis=1))
            b_high, b_low = split(jnp.concatenate(b_cols, axis=1))
            r.acc[...] += dot_nt(
                jnp.concatenate([a_high, a_high, a_low], axis=1),
                jnp.concatenate([b_high, b_low, b_high], axis=1),
            )
    folded = jnp.sum(jnp.where(same, r.acc[...], 0.0).reshape(32, 8, 256), axis=1)
    pick = (iota((256, 128), 0) // 8 == iota((256, 128), 1)).astype(F32).astype(BF16)
    fold_high, fold_low = split(folded)
    pointwise = dot(
        jnp.concatenate([fold_high, fold_low], axis=1), jnp.concatenate([pick, pick], axis=0)
    )
    dense = pointwise[0:8]
    for k in range(1, 4):
        dense = dense + roll(pointwise[8 * k : 8 * k + 8], 32 * k)
    sums = jnp.sum(r.gp[0], axis=1)
    for t in range(1, 4):
        sums = sums + jnp.sum(r.gp[t], axis=1)
    sum_high, sum_low = split(sums)
    ones = jnp.ones((8, 256), BF16)
    bias_row = dot_nt(
        ones,
        jnp.concatenate(
            [jnp.concatenate([sum_high, sum_low], axis=1), jnp.zeros((96, 256), BF16)], axis=0
        ),
    )
    for i in range(8):
        r.part1[i] = dense[i : i + 1]
    r.part1[8] = bias_row[0:1]


def weight_gradient(r):
    lane8 = iota((8, 128), 1)
    sign = jnp.where(lane8 // 32 % 2 == 0, 1.0, -1.0)
    low_half = lane8 < 64
    for q in range(16):
        s_q = r.s_all[pl.ds(q, 8, stride=16), :]
        g_q = r.g_all[pl.ds(q, 8, stride=16), :]
        first = s_q * sign
        second = jnp.where(lane8 // 32 % 2 == 0, roll(s_q, -32), roll(s_q, 32))
        left_rows = jnp.concatenate(
            [
                jnp.where(low_half, first, 0.0),
                jnp.where(low_half, second, 0.0),
                jnp.where(low_half, 0.0, first),
                jnp.where(low_half, 0.0, second),
            ],
            axis=0,
        )
        right_rows = jnp.concatenate([roll(g_q, -32 * g) for g in range(4)], axis=0)
        l_high, l_low = split(left_rows)
        r_high, r_low = split(right_rows)
        res = dot_tn(
            jnp.concatenate([l_high, l_high, l_low], axis=0),
            jnp.concatenate([r_high, r_low, r_high], axis=0),
        )
        r.gspec[pl.ds(q, 128, stride=16), :] = res[:, 0:32]


def final_cells(r, t):
    for pair in range(2):
        field = z_inverse(r, t, pair)
        for half in range(2):
            ob = 2 * pair + half
            r.res[t, pl.ds(ob * 8, 8)] = r.loc[t, pl.ds(ob * 8, 8)] + field[
                :, half * 128 : half * 128 + 128
            ].reshape(8, 32, 128)


CELLS, SLOTS = (4, 32, 32, 128), (64, 4, 128)
IN_NAMES = ["v", "w", "lw", "bias", "cot", "zf", "xf", "yf", "yi", "xi", "zi"]
OUT_SHAPES = dict(
    lay=(CELLS, F32), loc=(CELLS, F32), gspec=((2048, 32), F32), recv3=(SLOTS, F32),
    total=((16, 9, 1, 128), F32), xi=((384, 1024), BF16), zi=((256, 384), BF16),
)
SCRATCH = dict(
    v=(CELLS, F32), w=((2048, 32), F32), lw=((32, 32), F32), cot=(CELLS, F32),
    zf=((128, 768), BF16), xf=((64, 1536), BF16), yf=((128, 768), BF16), yi=((256, 384), BF16),
    modes=((4, 128, 512), F32), gp=(CELLS, F32),
    bw_high=((16, 128, 128), BF16), bw_low=((16, 128, 128), BF16),
    bwt_high=((16, 128, 128), BF16), bwt_low=((16, 128, 128), BF16),
    kron_f=((256, 768), BF16), kron_b=((256, 768), BF16),
    flat=((256, 128), F32), spread=((2, 128, 1024), F32),
    s_all=((128, 128), F32), g_all=((128, 128), F32), acc=((256, 256), F32),
    part1=((9, 1, 128), F32), stage1=((16, 9, 1, 128), F32), part2=((9, 1, 128), F32),
    shift=((32, 8, 128), F32),
    send0=(SLOTS, F32), send1=(SLOTS, F32), send2=(SLOTS, F32), send3=(SLOTS, F32),
    recv0=(SLOTS, F32), recv1=(SLOTS, F32), recv2=(SLOTS, F32),
)
SEMAPHORES = dict(in_sem=16, send_sem=6, recv_sem=6, small_send=2, small_recv=2)


def kernel(*refs):
    names = [n + "_hbm" for n in IN_NAMES]
    names += list(OUT_SHAPES) + list(SCRATCH) + ["bias"] + list(SEMAPHORES)
    r = types.SimpleNamespace(**dict(zip(names, refs, strict=True)))
    me = lax.axis_index("pencil")
    group = lax.axis_index("batch")
    my_y, my_x, my_z = me // 16, me // 4 % 4, me % 4
    across = (group + 2) % GROUPS

    def peer_of(dy, dx, to_z):
        return (my_y + dy) % 4 * 16 + (my_x + dx) % 4 * 4 + to_z

    barrier = pltpu.get_barrier_semaphore()
    for dy, dx in FAR_FIRST:
        for to_z in range(4):
            pl.semaphore_signal(
                barrier, inc=1, device_id=(across, peer_of(dy, dx, to_z)), device_id_type=MESH
            )
    greetings = PEERS
    around = []
    for dg in range(4):
        for dz in range(4):
            if dg == 0 and dz == 0:
                continue
            near = ((group + dg) % GROUPS, me - my_z + (my_z + dz) % 4)
            around.append(near)
            if dg != 2:
                greetings += 1
                pl.semaphore_signal(barrier, inc=1, device_id=near, device_id_type=MESH)

    for dy, dx in FAR_FIRST[:-1]:
        greetings += 1
        pl.semaphore_signal(
            barrier, inc=1, device_id=(group, peer_of(dy, dx, my_z)), device_id_type=MESH
        )

    loads = {}

    def load(name, src, dst):
        loads[name] = pltpu.make_async_copy(src, dst, r.in_sem.at[len(loads)])
        loads[name].start()

    load("zf", r.zf_hbm, r.zf)
    for t in range(4):
        load("v%d" % t, r.v_hbm.at[t], r.v.at[t])
    for name in ("xf", "bias", "lw", "w", "yf", "yi", "xi", "zi", "cot"):
        load(name, getattr(r, name + "_hbm"), getattr(r, name))

    def send_to(send, recv, index):
        def dispatch(to_z):
            for dy, dx in FAR_FIRST:
                peer = peer_of(dy, dx, to_z)
                pltpu.make_async_remote_copy(
                    src_ref=send.at[to_z * 16 + peer // 4],
                    dst_ref=recv.at[me],
                    send_sem=r.send_sem.at[index],
                    recv_sem=r.recv_sem.at[index],
                    device_id=(across, peer),
                    device_id_type=MESH,
                ).start()

        return dispatch

    def await_bytes(ref, sem):
        pltpu.make_async_copy(ref, ref, sem).wait()

    own = pl.ds(pl.multiple_of(group * 32, 32), 32)

    def share(buffer, index):
        for dg in (2, 1, 3):
            pltpu.make_async_remote_copy(
                src_ref=buffer.at[own],
                dst_ref=buffer.at[own],
                send_sem=r.send_sem.at[index],
                recv_sem=r.recv_sem.at[index],
                device_id=((group + dg) % GROUPS, me),
                device_id_type=MESH,
            ).start()

    spot = group * 4 + my_z
    fifteen = pl.ds(0, 15)

    loads["zf"].wait()
    for t in range(4):
        loads["v%d" % t].wait()
        field_modes(r, r.v, t)
    loads["xf"].wait()
    x_forward(r, r.send0, lambda to_z: None)
    pl.semaphore_wait(barrier, greetings)
    for to_z in Z_ORDER:
        send_to(r.send0, r.recv0, 0)(to_z)

    loads["lw"].wait()
    loads["bias"].wait()
    pointwise_tables(r)
    loads["w"].wait()
    mode_tables(r)
    channel_mix(r.kron_f, r.v, r.loc, r.shift)

    loads["yf"].wait()
    loads["yi"].wait()
    await_bytes(r.recv0, r.recv_sem.at[0])
    mix(r, own, send_to(r.send1, r.recv1, 1))

    loads["xi"].wait()
    loads["zi"].wait()
    loads["cot"].wait()
    await_bytes(r.recv1, r.recv_sem.at[1])
    share(r.s_all, 4)
    x_inverse(r, r.recv1)
    for t in range(4):
        cells(r, t)
    for t in range(4):
        field_modes(r, r.gp, t)
    x_forward(r, r.send2, send_to(r.send2, r.recv2, 2))

    point_sums(r)
    for dy, dx in FAR_FIRST[:-1]:
        pltpu.make_async_remote_copy(
            src_ref=r.part1,
            dst_ref=r.stage1.at[me // 4],
            send_sem=r.small_send.at[0],
            recv_sem=r.small_recv.at[0],
            device_id=(group, peer_of(dy, dx, my_z)),
            device_id_type=MESH,
        ).start()
    r.stage1[me // 4] = r.part1[...]
    channel_mix(r.kron_b, r.gp, r.loc)

    await_bytes(r.recv2, r.recv_sem.at[2])
    await_bytes(r.stage1.at[fifteen], r.small_recv.at[0])
    r.part2[...] = jnp.sum(r.stage1[...], axis=0)
    for to_group, to_peer in around:
        pltpu.make_async_remote_copy(
            src_ref=r.part2,
            dst_ref=r.total.at[spot],
            send_sem=r.small_send.at[1],
            recv_sem=r.small_recv.at[1],
            device_id=(to_group, to_peer),
            device_id_type=MESH,
        ).start()
    r.total[spot] = r.part2[...]
    mix_adjoint(r, own, send_to(r.send3, r.recv3, 3), lambda: share(r.g_all, 5))

    for buffer, index in ((r.s_all, 4), (r.g_all, 5)):
        await_bytes(buffer.at[pl.ds(0, 96)], r.recv_sem.at[index])
    weight_gradient(r)

    for index, buffer in enumerate((r.send0, r.send1, r.send2, r.send3)):
        await_bytes(buffer, r.send_sem.at[index])
    for index, buffer in ((4, r.s_all), (5, r.g_all)):
        await_bytes(buffer.at[pl.ds(0, 96)], r.send_sem.at[index])
    await_bytes(r.stage1.at[fifteen], r.small_send.at[0])
    await_bytes(r.total.at[fifteen], r.small_send.at[1])
    await_bytes(r.total.at[fifteen], r.small_recv.at[1])
    await_bytes(r.recv3, r.recv_sem.at[3])


TAIL_SCRATCH = dict(
    flat=((256, 128), F32), spread=((2, 128, 1024), F32), res=(CELLS, F32),
)


def tail(*refs):
    names = list(OUT_SHAPES) + ["layer_out", "grad_state", "grad_spectral", "grad_local", "grad_bias"]
    names += list(TAIL_SCRATCH) + ["sem"]
    r = types.SimpleNamespace(**dict(zip(names, refs, strict=True)))
    copies = []

    def copy(src, dst):
        copies.append(pltpu.make_async_copy(src, dst, r.sem.at[len(copies)]))
        copies[-1].start()

    copy(r.lay, r.layer_out)
    copy(r.gspec, r.grad_spectral)
    total = jnp.sum(r.total[...], axis=0).reshape(9, 128) * (1.0 / math.sqrt(8 * X * Y * Z))
    for k in range(4):
        r.grad_local[pl.ds(8 * k, 8), :] = roll(total[0:8], -32 * k)[:, 0:32]
    r.grad_bias[...] = total[8:9, 0:32]
    x_inverse(r, r.recv3)
    for t in range(4):
        final_cells(r, t)
        copy(r.res.at[t], r.grad_state.at[t])
    for pending in copies:
        pending.wait()


def vmem(array):
    return pltpu.with_memory_space_constraint(array, pltpu.VMEM)


def hbm(array):
    return pltpu.with_memory_space_constraint(array, pltpu.HBM)


def shards(state_field, spectral_weight, local_weight, channel_bias, cotangent):
    tables = [hbm(jnp.asarray(t)) for t in build_tables()]
    in_hbm = pl.BlockSpec(memory_space=pltpu.HBM)
    in_vmem = pl.BlockSpec(memory_space=pltpu.VMEM)
    held = pl.pallas_call(
        kernel,
        out_shape=tuple(pltpu.VMEM(*s) for s in OUT_SHAPES.values()),
        in_specs=[in_hbm] * len(IN_NAMES),
        out_specs=(in_vmem,) * len(OUT_SHAPES),
        scratch_shapes=[pltpu.VMEM(*s) for s in SCRATCH.values()]
        + [pltpu.SMEM((32,), F32)]
        + [pltpu.SemaphoreType.DMA((n,)) for n in SEMAPHORES.values()],
        compiler_params=pltpu.CompilerParams(
            collective_id=0, has_side_effects=True, vmem_limit_bytes=40 * 1024 * 1024
        ),
        name="fno_layer",
    )(
        hbm(state_field.reshape(CELLS)),
        hbm(jnp.swapaxes(spectral_weight, 3, 4).reshape(2048, 32)),
        hbm(local_weight),
        hbm(channel_bias),
        hbm(cotangent.reshape(CELLS)),
        *tables,
    )
    out = pl.pallas_call(
        tail,
        out_shape=(
            jax.ShapeDtypeStruct(CELLS, F32),
            jax.ShapeDtypeStruct(CELLS, F32),
            jax.ShapeDtypeStruct((2048, 32), F32),
            jax.ShapeDtypeStruct((32, 32), F32),
            jax.ShapeDtypeStruct((1, 32), F32),
        ),
        in_specs=[in_vmem] * len(OUT_SHAPES),
        out_specs=(in_hbm, in_hbm, in_hbm, in_vmem, in_vmem),
        scratch_shapes=[pltpu.VMEM(*s) for s in TAIL_SCRATCH.values()]
        + [pltpu.SemaphoreType.DMA((6,))],
        compiler_params=pltpu.CompilerParams(vmem_limit_bytes=24 * 1024 * 1024),
        name="fno_tail",
    )(*[vmem(h) for h in held])
    layer_out, grad_state, grad_spectral, grad_local, grad_bias = out
    return (
        layer_out.reshape(state_field.shape),
        grad_state.reshape(state_field.shape),
        jnp.swapaxes(grad_spectral.reshape(2, 2, 32, 16, 32), 3, 4),
        grad_local,
        grad_bias.reshape(32),
    )


def solution(mesh):
    cells = P("batch", "pencil", None, None, None)
    modes = P("pencil", None, None, None, None)
    return jax.shard_map(
        shards,
        mesh=mesh,
        in_specs=(cells, modes, P(), P(), cells),
        out_specs=(cells, cells, modes, P(), P()),
        check_vma=False,
    )
```

```python
import math
import types

import jax
import jax.numpy as jnp
import ml_dtypes
import numpy as np
from jax import lax
from jax.experimental import pallas as pl
from jax.experimental.pallas import tpu as pltpu
from jax.sharding import PartitionSpec as P

X, Y, Z, C = 128, 128, 32, 32
MX, MY, MZ = 16, 16, 8
PEERS, GROUPS = 64, 4
F32, BF16 = jnp.float32, jnp.bfloat16
gelu_scale = math.sqrt(2.0 / math.pi)
cubic_term = 0.044715
MESH = pl.DeviceIdType.MESH


def angles(points, kept_modes):
    order = np.arange(kept_modes)
    frequency = np.where(order < kept_modes // 2, order, points - kept_modes + order)
    phases = (np.arange(points)[:, None] * frequency[None, :]) % points
    theta = phases * (2.0 * np.pi / points)
    return np.cos(theta), np.sin(theta)


def halves(table):
    table = table.astype(np.float32)
    high = table.astype(ml_dtypes.bfloat16)
    low = (table - high.astype(np.float32)).astype(ml_dtypes.bfloat16)
    return high, low


def left(table):
    high, low = halves(table)
    return np.concatenate([high, low, high], axis=1)


def build_tables():
    cos_x, sin_x = angles(X, MX)
    cos_y, sin_y = angles(Y, MY)
    cos_z, sin_z = angles(Z, MZ)
    scaling = 1.0 / math.sqrt(X * Y * Z)
    zf = np.stack([cos_z.T, -sin_z.T], axis=1)
    zf = np.einsum("krz,cd->krcdz", zf, np.eye(8)).reshape(128, 256)
    xf = np.stack(
        [np.stack([cos_x.T, sin_x.T], 1), np.stack([-sin_x.T, cos_x.T], 1)], 1
    )
    xf = np.einsum("kabx,pq->kapqbx", xf, np.eye(2)).reshape(64, 512) * scaling
    cy = cos_y.reshape(64, 2, 16)
    sy = sin_y.reshape(64, 2, 16)
    yf = np.stack([np.stack([cy, sy], 0), np.stack([-sy, cy], 0)], 0)
    yf = np.einsum("abpyq,mn->ymaqpbn", yf, np.eye(2)).reshape(128, 256)
    xi = np.stack(
        [np.stack([cos_x.T, sin_x.T], 1), np.stack([-sin_x.T, cos_x.T], 1)], 0
    )
    xi = np.einsum("akbx,mn->maknbx", xi, np.eye(2)).reshape(64, 512) * scaling
    xi_high, xi_low = halves(xi)
    return (
        left(zf),
        left(xf),
        left(yf),
        left(yf.T.reshape(16, 4, 4, 128).swapaxes(0, 1).reshape(256, 128)),
        np.concatenate([xi_high, xi_low, xi_high], axis=0),
        left(zf.T),
    )


Z_ORDER = (0, 2, 1, 3)
RING = (0, 1, 2, 1)
FAR_FIRST = sorted(
    ((dy, dx) for dy in range(4) for dx in range(4)), key=lambda d: -RING[d[0]] - RING[d[1]]
)


def split(value):
    high = value.astype(BF16)
    return high, (value - high.astype(F32)).astype(BF16)


def rows_of(value):
    high, low = split(value)
    return jnp.concatenate([high, high, low], axis=0)


def lanes_of(value):
    high, low = split(value)
    return jnp.concatenate([high, high, low], axis=1)


def dot(a, b):
    return jnp.dot(a, b, preferred_element_type=F32)


def dot_nt(a, b):
    return lax.dot_general(a, b, (((1,), (1,)), ((), ())), preferred_element_type=F32)


def dot_tn(a, b):
    return lax.dot_general(a, b, (((0,), (0,)), ((), ())), preferred_element_type=F32)


def iota(shape, dim):
    return lax.broadcasted_iota(jnp.int32, shape, dim)


def roll(value, shift):
    shift = shift % value.shape[1]
    return value if shift == 0 else pltpu.roll(value, shift, 1)


def z_forward(r, block2, t, pair):
    res = dot(r.zf[...], rows_of(block2))
    order = (t % 2) * 2 + t // 2
    for half in range(2):
        row = order * 32 + (2 * pair + half) * 8
        for kz in range(8):
            for ri in range(2):
                k = kz * 2 + ri
                r.modes[kz // 2, pl.ds(row, 8), pl.ds(((kz % 2) * 2 + ri) * 128, 128)] = res[
                    k * 8 : k * 8 + 8, half * 128 : half * 128 + 128
                ]


def x_forward(r, send, dispatch):
    for kzp in Z_ORDER:
        res = dot_nt(r.xf[...], lanes_of(r.modes[kzp]))
        send[kzp * 16 : kzp * 16 + 16] = res.reshape(16, 4, 128)
        dispatch(kzp)


def y_forward(r, recv):
    lane = iota((16, 128), 1)
    got = recv[...].reshape(256, 128)
    res = dot(r.yf[...], rows_of(got))
    res = res[0:64] + roll(res[64:128], 64)
    rows = []
    for b in range(2):
        total = jnp.zeros((16, 128), F32)
        for g in range(4):
            piece = roll(res[g * 16 : g * 16 + 16], (g - b) * 32)
            total = jnp.where(lane // 32 == g, piece, total)
        rows.append(total)
    return jnp.concatenate(rows, axis=0)


def y_inverse(r, value, send, dispatch):
    lane = iota((16, 128), 1)
    tops = []
    for g in range(4):
        first = roll(value[0:16], -g * 32)
        second = roll(value[16:32], (1 - g) * 32)
        tops.append(jnp.where(lane < 32, first, jnp.where(lane < 64, second, 0.0)))
    top = jnp.concatenate(tops, axis=0)
    both = jnp.concatenate([top, roll(top, 64)], axis=0)
    both = rows_of(both)
    for to_z in Z_ORDER:
        res = dot(r.yi[to_z * 64 : to_z * 64 + 64, :], both)
        send[to_z * 16 : to_z * 16 + 16] = res.reshape(16, 4, 128)
        dispatch(to_z)


def masked(parts, j):
    row_q = iota((32, 128), 0) % 16
    picks = [row_q == 2 * j, row_q == 2 * j + 1]

    def pick(part):
        wide = part.astype(F32)
        return jnp.concatenate(
            [jnp.where(p, wide, 0.0).astype(BF16) for p in picks], axis=1
        )

    return pick(parts[0]), pick(parts[1])


def x_inverse(r, recv):
    r.flat[...] = recv[...].reshape(256, 128)
    for g in range(4):
        pieces = []
        for k2 in range(2):
            for ri in range(2):
                pieces.append(r.flat[pl.ds(g * 4 + ri * 2 + k2, 16, stride=16), :])
        block = rows_of(jnp.concatenate(pieces, axis=0))
        r.spread[g // 2, :, g % 2 * 512 : g % 2 * 512 + 512] = dot_tn(block, r.xi[...])


def z_inverse(r, t, pair):
    order = (t % 2) * 2 + t // 2
    columns = []
    for half in range(2):
        row = order * 32 + (2 * pair + half) * 8
        tiles = []
        for k in range(16):
            tiles.append(r.spread[k // 8, pl.ds(row, 8), pl.ds((k % 8) * 128, 128)])
        columns.append(jnp.concatenate(tiles, axis=0))
    block = jnp.concatenate(columns, axis=1)
    return dot(r.zi[...], rows_of(block))


def channel_mix(table, src, dst, shift=None):
    for t in range(4):
        for pair in range(2):
            cols = []
            for half in range(2):
                zb = 2 * pair + half
                cols.append(src[t, :, pl.ds(zb * 8, 8), :].reshape(256, 128))
            res = dot(table[...], rows_of(jnp.concatenate(cols, axis=1)))
            for half in range(2):
                zb = 2 * pair + half
                part = res[:, half * 128 : half * 128 + 128].reshape(32, 8, 128)
                if shift is not None:
                    part = part + shift[...]
                dst[t, :, pl.ds(zb * 8, 8), :] = part


def pair_of(src, t, pair):
    return jnp.concatenate(
        [src[t, pl.ds((2 * pair + half) * 8, 8)].reshape(256, 128) for half in range(2)],
        axis=1,
    )


def field_modes(r, field, t):
    for pair in range(2):
        z_forward(r, pair_of(field, t, pair), t, pair)


def same_z():
    return iota((256, 256), 0) % 8 == iota((256, 256), 1) % 8


def pointwise_tables(r):
    expand = (iota((256, 32), 0) // 8 == iota((256, 32), 1)).astype(F32).astype(BF16)
    same = same_z()
    lw_high, lw_low = split(r.lw[...])
    for i, part_of in enumerate((lw_high, lw_low, lw_high)):
        once = dot_nt(expand, part_of).astype(BF16)
        r.kron_f[:, pl.ds(i * 256, 256)] = jnp.where(same, dot_nt(once, expand), 0.0).astype(BF16)
        once = dot(expand, part_of).astype(BF16)
        r.kron_b[:, pl.ds(i * 256, 256)] = jnp.where(same, dot_nt(once, expand), 0.0).astype(BF16)


    for o in range(32):
        r.shift[o] = jnp.full((8, 128), r.bias[o], F32)


def mode_tables(r):
    zeros = jnp.zeros((32, 32), F32)
    for q in range(16):
        rows = []
        for m in range(2):
            real = r.w[pl.ds((m * 2 + 0) * 512 + q, 32, stride=16), :]
            imag = r.w[pl.ds((m * 2 + 1) * 512 + q, 32, stride=16), :]
            for ri, pieces in enumerate(((real, imag), (-imag, real))):
                pieces = list(pieces)
                both = pieces + [zeros, zeros] if m == 0 else [zeros, zeros] + pieces
                rows.append(jnp.concatenate(both, axis=1))
        block = jnp.concatenate(rows, axis=0)
        r.bw_high[q], r.bw_low[q] = split(block)
        r.bwt_high[q], r.bwt_low[q] = split(block.T)


def all_modes(value, right_high, right_low):
    parts = split(value)
    lefts = [masked(parts, j) for j in range(8)]
    high = jnp.concatenate([l[0] for l in lefts], axis=1)
    low = jnp.concatenate([l[1] for l in lefts], axis=1)
    r_high = right_high[...].reshape(2048, 128)
    r_low = right_low[...].reshape(2048, 128)
    both = dot(jnp.concatenate([high, low], axis=0), r_high)
    return both[0:32] + both[32:64] + dot(high, r_low)


def mix(r, own, dispatch):
    spectrum = y_forward(r, r.recv0)
    r.s_all[own, :] = spectrum
    mixed = all_modes(spectrum, r.bw_high, r.bw_low)
    y_inverse(r, mixed, r.send1, dispatch)


def mix_adjoint(r, own, dispatch):
    grad_modes = y_forward(r, r.recv2)
    r.g_all[own, :] = grad_modes
    back = all_modes(grad_modes, r.bwt_high, r.bwt_low)
    y_inverse(r, back, r.send3, dispatch)


def cells(r, t):
    for pair in range(2):
        field = z_inverse(r, t, pair)
        for half in range(2):
            for o8 in range(8):
                o = (2 * pair + half) * 8 + o8
                pre = field[o8 * 32 : o8 * 32 + 32, half * 128 : half * 128 + 128] + r.loc[t, o]
                square = pre * pre
                bent = jnp.tanh(pre * (gelu_scale + (gelu_scale * cubic_term) * square))
                half_up = 0.5 + 0.5 * bent
                r.lay[t, o] = pre * half_up
                rise = (0.5 * gelu_scale) + (1.5 * gelu_scale * cubic_term) * square
                slope = half_up + (pre * rise) * (1.0 - bent * bent)
                grad = r.cot[t, o] * slope
                r.gp[t, o] = grad


def point_sums(r):
    same = same_z()
    r.acc[...] = jnp.zeros((256, 256), F32)
    for t in range(4):
        for pair in range(2):
            a_cols, b_cols = [], []
            for half in range(2):
                zb = 2 * pair + half
                a_cols.append(r.v[t, :, pl.ds(zb * 8, 8), :].reshape(256, 128))
                b_cols.append(r.gp[t, :, pl.ds(zb * 8, 8), :].reshape(256, 128))
            a_high, a_low = split(jnp.concatenate(a_cols, axis=1))
            b_high, b_low = split(jnp.concatenate(b_cols, axis=1))
            r.acc[...] += dot_nt(
                jnp.concatenate([a_high, a_high, a_low], axis=1),
                jnp.concatenate([b_high, b_low, b_high], axis=1),
            )
    folded = jnp.sum(jnp.where(same, r.acc[...], 0.0).reshape(32, 8, 256), axis=1)
    pick = (iota((256, 128), 0) // 8 == iota((256, 128), 1)).astype(F32).astype(BF16)
    fold_high, fold_low = split(folded)
    pointwise = dot(
        jnp.concatenate([fold_high, fold_low], axis=1), jnp.concatenate([pick, pick], axis=0)
    )
    dense = pointwise[0:8]
    for k in range(1, 4):
        dense = dense + roll(pointwise[8 * k : 8 * k + 8], 32 * k)
    sums = jnp.sum(r.gp[0], axis=1)
    for t in range(1, 4):
        sums = sums + jnp.sum(r.gp[t], axis=1)
    sum_high, sum_low = split(sums)
    ones = jnp.ones((8, 256), BF16)
    bias_row = dot_nt(
        ones,
        jnp.concatenate(
            [jnp.concatenate([sum_high, sum_low], axis=1), jnp.zeros((96, 256), BF16)], axis=0
        ),
    )
    for i in range(8):
        r.part1[i] = dense[i : i + 1]
    r.part1[8] = bias_row[0:1]


def weight_gradient(r):
    lane8 = iota((8, 128), 1)
    sign = jnp.where(lane8 // 32 % 2 == 0, 1.0, -1.0)
    low_half = lane8 < 64
    for q in range(16):
        s_q = r.s_all[pl.ds(q, 8, stride=16), :]
        g_q = r.g_all[pl.ds(q, 8, stride=16), :]
        first = s_q * sign
        second = jnp.where(lane8 // 32 % 2 == 0, roll(s_q, -32), roll(s_q, 32))
        left_rows = jnp.concatenate(
            [
                jnp.where(low_half, first, 0.0),
                jnp.where(low_half, second, 0.0),
                jnp.where(low_half, 0.0, first),
                jnp.where(low_half, 0.0, second),
            ],
            axis=0,
        )
        right_rows = jnp.concatenate([roll(g_q, -32 * g) for g in range(4)], axis=0)
        l_high, l_low = split(left_rows)
        r_high, r_low = split(right_rows)
        res = dot_tn(
            jnp.concatenate([l_high, l_high, l_low], axis=0),
            jnp.concatenate([r_high, r_low, r_high], axis=0),
        )
        r.gspec[pl.ds(q, 128, stride=16), :] = res[:, 0:32]


def final_cells(r, t):
    for pair in range(2):
        field = z_inverse(r, t, pair)
        for half in range(2):
            ob = 2 * pair + half
            r.res[t, pl.ds(ob * 8, 8)] = r.loc[t, pl.ds(ob * 8, 8)] + field[
                :, half * 128 : half * 128 + 128
            ].reshape(8, 32, 128)


CELLS, SLOTS = (4, 32, 32, 128), (64, 4, 128)
IN_NAMES = ["v", "w", "lw", "bias", "cot", "zf", "xf", "yf", "yi", "xi", "zi"]
OUT_SHAPES = dict(
    lay=(CELLS, F32), loc=(CELLS, F32), s_all=((128, 128), F32), g_all=((128, 128), F32), recv3=(SLOTS, F32),
    total=((16, 9, 1, 128), F32), xi=((192, 512), BF16), zi=((256, 384), BF16),
)
SCRATCH = dict(
    v=(CELLS, F32), w=((2048, 32), F32), lw=((32, 32), F32), cot=(CELLS, F32),
    zf=((128, 768), BF16), xf=((64, 1536), BF16), yf=((128, 768), BF16), yi=((256, 384), BF16),
    modes=((4, 128, 512), F32), gp=(CELLS, F32),
    bw_high=((16, 128, 128), BF16), bw_low=((16, 128, 128), BF16),
    bwt_high=((16, 128, 128), BF16), bwt_low=((16, 128, 128), BF16),
    kron_f=((256, 768), BF16), kron_b=((256, 768), BF16),
    flat=((256, 128), F32), spread=((2, 128, 1024), F32),
    acc=((256, 256), F32),
    part1=((9, 1, 128), F32), stage1=((16, 9, 1, 128), F32), part2=((9, 1, 128), F32),
    shift=((32, 8, 128), F32),
    send0=(SLOTS, F32), send1=(SLOTS, F32), send2=(SLOTS, F32), send3=(SLOTS, F32),
    recv0=(SLOTS, F32), recv1=(SLOTS, F32), recv2=(SLOTS, F32),
)
SEMAPHORES = dict(in_sem=16, send_sem=6, recv_sem=6, small_send=2, small_recv=2)


def kernel(*refs):
    names = [n + "_hbm" for n in IN_NAMES]
    names += list(OUT_SHAPES) + list(SCRATCH) + ["bias"] + list(SEMAPHORES)
    r = types.SimpleNamespace(**dict(zip(names, refs, strict=True)))
    me = lax.axis_index("pencil")
    group = lax.axis_index("batch")
    my_y, my_x, my_z = me // 16, me // 4 % 4, me % 4
    across = (group + 2) % GROUPS

    def peer_of(dy, dx, to_z):
        return (my_y + dy) % 4 * 16 + (my_x + dx) % 4 * 4 + to_z

    barrier = pltpu.get_barrier_semaphore()
    for dy, dx in FAR_FIRST:
        for to_z in range(4):
            pl.semaphore_signal(
                barrier, inc=1, device_id=(across, peer_of(dy, dx, to_z)), device_id_type=MESH
            )
    greetings = PEERS
    around = []
    for dg in range(4):
        for dz in range(4):
            if dg == 0 and dz == 0:
                continue
            near = ((group + dg) % GROUPS, me - my_z + (my_z + dz) % 4)
            around.append(near)
            if dg != 2:
                greetings += 1
                pl.semaphore_signal(barrier, inc=1, device_id=near, device_id_type=MESH)

    for dy, dx in FAR_FIRST[:-1]:
        greetings += 1
        pl.semaphore_signal(
            barrier, inc=1, device_id=(group, peer_of(dy, dx, my_z)), device_id_type=MESH
        )

    loads = {}

    def load(name, src, dst):
        loads[name] = pltpu.make_async_copy(src, dst, r.in_sem.at[len(loads)])
        loads[name].start()

    load("zf", r.zf_hbm, r.zf)
    for t in range(4):
        load("v%d" % t, r.v_hbm.at[t], r.v.at[t])
    for name in ("xf", "bias", "lw", "w", "yf", "yi", "xi", "zi", "cot"):
        load(name, getattr(r, name + "_hbm"), getattr(r, name))

    def send_to(send, recv, index):
        def dispatch(to_z):
            for dy, dx in FAR_FIRST:
                peer = peer_of(dy, dx, to_z)
                pltpu.make_async_remote_copy(
                    src_ref=send.at[to_z * 16 + peer // 4],
                    dst_ref=recv.at[me],
                    send_sem=r.send_sem.at[index],
                    recv_sem=r.recv_sem.at[index],
                    device_id=(across, peer),
                    device_id_type=MESH,
                ).start()

        return dispatch

    def await_bytes(ref, sem):
        pltpu.make_async_copy(ref, ref, sem).wait()

    own = pl.ds(pl.multiple_of(group * 32, 32), 32)

    def share(buffer, index):
        for dg in (2, 1, 3):
            pltpu.make_async_remote_copy(
                src_ref=buffer.at[own],
                dst_ref=buffer.at[own],
                send_sem=r.send_sem.at[index],
                recv_sem=r.recv_sem.at[index],
                device_id=((group + dg) % GROUPS, me),
                device_id_type=MESH,
            ).start()

    spot = group * 4 + my_z
    fifteen = pl.ds(0, 15)

    loads["zf"].wait()
    for t in range(4):
        loads["v%d" % t].wait()
        field_modes(r, r.v, t)
    loads["xf"].wait()
    x_forward(r, r.send0, lambda to_z: None)
    pl.semaphore_wait(barrier, greetings)
    for to_z in Z_ORDER:
        send_to(r.send0, r.recv0, 0)(to_z)

    loads["lw"].wait()
    loads["bias"].wait()
    pointwise_tables(r)
    loads["w"].wait()
    mode_tables(r)
    channel_mix(r.kron_f, r.v, r.loc, r.shift)

    loads["yf"].wait()
    loads["yi"].wait()
    await_bytes(r.recv0, r.recv_sem.at[0])
    mix(r, own, send_to(r.send1, r.recv1, 1))

    loads["xi"].wait()
    loads["zi"].wait()
    loads["cot"].wait()
    await_bytes(r.recv1, r.recv_sem.at[1])
    share(r.s_all, 4)
    x_inverse(r, r.recv1)
    for t in range(4):
        cells(r, t)
    for t in range(4):
        field_modes(r, r.gp, t)
    x_forward(r, r.send2, send_to(r.send2, r.recv2, 2))

    point_sums(r)
    for dy, dx in FAR_FIRST[:-1]:
        pltpu.make_async_remote_copy(
            src_ref=r.part1,
            dst_ref=r.stage1.at[me // 4],
            send_sem=r.small_send.at[0],
            recv_sem=r.small_recv.at[0],
            device_id=(group, peer_of(dy, dx, my_z)),
            device_id_type=MESH,
        ).start()
    r.stage1[me // 4] = r.part1[...]
    channel_mix(r.kron_b, r.gp, r.loc)

    await_bytes(r.recv2, r.recv_sem.at[2])
    await_bytes(r.stage1.at[fifteen], r.small_recv.at[0])
    r.part2[...] = jnp.sum(r.stage1[...], axis=0)
    for to_group, to_peer in around:
        pltpu.make_async_remote_copy(
            src_ref=r.part2,
            dst_ref=r.total.at[spot],
            send_sem=r.small_send.at[1],
            recv_sem=r.small_recv.at[1],
            device_id=(to_group, to_peer),
            device_id_type=MESH,
        ).start()
    r.total[spot] = r.part2[...]
    mix_adjoint(r, own, send_to(r.send3, r.recv3, 3))
    share(r.g_all, 5)

    for buffer, index in ((r.s_all, 4), (r.g_all, 5)):
        await_bytes(buffer.at[pl.ds(0, 96)], r.recv_sem.at[index])

    for index, buffer in enumerate((r.send0, r.send1, r.send2, r.send3)):
        await_bytes(buffer, r.send_sem.at[index])
    for index, buffer in ((4, r.s_all), (5, r.g_all)):
        await_bytes(buffer.at[pl.ds(0, 96)], r.send_sem.at[index])
    await_bytes(r.stage1.at[fifteen], r.small_send.at[0])
    await_bytes(r.total.at[fifteen], r.small_send.at[1])
    await_bytes(r.total.at[fifteen], r.small_recv.at[1])
    await_bytes(r.recv3, r.recv_sem.at[3])


TAIL_SCRATCH = dict(
    flat=((256, 128), F32), spread=((2, 128, 1024), F32), res=(CELLS, F32), gspec=((2048, 32), F32),
)


def tail(*refs):
    names = list(OUT_SHAPES) + ["layer_out", "grad_state", "grad_spectral", "grad_local", "grad_bias"]
    names += list(TAIL_SCRATCH) + ["sem"]
    r = types.SimpleNamespace(**dict(zip(names, refs, strict=True)))
    copies = []

    def copy(src, dst):
        copies.append(pltpu.make_async_copy(src, dst, r.sem.at[len(copies)]))
        copies[-1].start()

    copy(r.lay, r.layer_out)
    weight_gradient(r)
    copy(r.gspec, r.grad_spectral)
    total = jnp.sum(r.total[...], axis=0).reshape(9, 128) * (1.0 / math.sqrt(8 * X * Y * Z))
    for k in range(4):
        r.grad_local[pl.ds(8 * k, 8), :] = roll(total[0:8], -32 * k)[:, 0:32]
    r.grad_bias[...] = total[8:9, 0:32]
    x_inverse(r, r.recv3)
    for t in range(4):
        final_cells(r, t)
        copy(r.res.at[t], r.grad_state.at[t])
    for pending in copies:
        pending.wait()


def vmem(array):
    return pltpu.with_memory_space_constraint(array, pltpu.VMEM)


def hbm(array):
    return pltpu.with_memory_space_constraint(array, pltpu.HBM)


def shards(state_field, spectral_weight, local_weight, channel_bias, cotangent):
    tables = [hbm(jnp.asarray(t)) for t in build_tables()]
    in_hbm = pl.BlockSpec(memory_space=pltpu.HBM)
    in_vmem = pl.BlockSpec(memory_space=pltpu.VMEM)
    held = pl.pallas_call(
        kernel,
        out_shape=tuple(pltpu.VMEM(*s) for s in OUT_SHAPES.values()),
        in_specs=[in_hbm] * len(IN_NAMES),
        out_specs=(in_vmem,) * len(OUT_SHAPES),
        scratch_shapes=[pltpu.VMEM(*s) for s in SCRATCH.values()]
        + [pltpu.SMEM((32,), F32)]
        + [pltpu.SemaphoreType.DMA((n,)) for n in SEMAPHORES.values()],
        compiler_params=pltpu.CompilerParams(
            collective_id=0, has_side_effects=True, vmem_limit_bytes=40 * 1024 * 1024
        ),
        name="fno_layer",
    )(
        hbm(state_field.reshape(CELLS)),
        hbm(jnp.swapaxes(spectral_weight, 3, 4).reshape(2048, 32)),
        hbm(local_weight),
        hbm(channel_bias),
        hbm(cotangent.reshape(CELLS)),
        *tables,
    )
    out = pl.pallas_call(
        tail,
        out_shape=(
            jax.ShapeDtypeStruct(CELLS, F32),
            jax.ShapeDtypeStruct(CELLS, F32),
            jax.ShapeDtypeStruct((2048, 32), F32),
            jax.ShapeDtypeStruct((32, 32), F32),
            jax.ShapeDtypeStruct((1, 32), F32),
        ),
        in_specs=[in_vmem] * len(OUT_SHAPES),
        out_specs=(in_hbm, in_hbm, in_hbm, in_vmem, in_vmem),
        scratch_shapes=[pltpu.VMEM(*s) for s in TAIL_SCRATCH.values()]
        + [pltpu.SemaphoreType.DMA((6,))],
        compiler_params=pltpu.CompilerParams(vmem_limit_bytes=24 * 1024 * 1024),
        name="fno_tail",
    )(*[vmem(h) for h in held])
    layer_out, grad_state, grad_spectral, grad_local, grad_bias = out
    return (
        layer_out.reshape(state_field.shape),
        grad_state.reshape(state_field.shape),
        jnp.swapaxes(grad_spectral.reshape(2, 2, 32, 16, 32), 3, 4),
        grad_local,
        grad_bias.reshape(32),
    )


def solution(mesh):
    cells = P("batch", "pencil", None, None, None)
    modes = P("pencil", None, None, None, None)
    return jax.shard_map(
        shards,
        mesh=mesh,
        in_specs=(cells, modes, P(), P(), cells),
        out_specs=(cells, cells, modes, P(), P()),
        check_vma=False,
    )
```

```python
import math
import types

import jax
import jax.numpy as jnp
import ml_dtypes
import numpy as np
from jax import lax
from jax.experimental import pallas as pl
from jax.experimental.pallas import tpu as pltpu
from jax.sharding import PartitionSpec as P

X, Y, Z, C = 128, 128, 32, 32
MX, MY, MZ = 16, 16, 8
PEERS, GROUPS = 64, 4
F32, BF16 = jnp.float32, jnp.bfloat16
gelu_scale = math.sqrt(2.0 / math.pi)
cubic_term = 0.044715
MESH = pl.DeviceIdType.MESH


def angles(points, kept_modes):
    order = np.arange(kept_modes)
    frequency = np.where(order < kept_modes // 2, order, points - kept_modes + order)
    phases = (np.arange(points)[:, None] * frequency[None, :]) % points
    theta = phases * (2.0 * np.pi / points)
    return np.cos(theta), np.sin(theta)


def halves(table):
    table = table.astype(np.float32)
    high = table.astype(ml_dtypes.bfloat16)
    low = (table - high.astype(np.float32)).astype(ml_dtypes.bfloat16)
    return high, low


def left(table):
    high, low = halves(table)
    return np.concatenate([high, low, high], axis=1)


def build_tables():
    cos_x, sin_x = angles(X, MX)
    cos_y, sin_y = angles(Y, MY)
    cos_z, sin_z = angles(Z, MZ)
    scaling = 1.0 / math.sqrt(X * Y * Z)
    zf = np.stack([cos_z.T, -sin_z.T], axis=1)
    zf = np.einsum("krz,cd->krcdz", zf, np.eye(8)).reshape(128, 256)
    xf = np.stack(
        [np.stack([cos_x.T, sin_x.T], 1), np.stack([-sin_x.T, cos_x.T], 1)], 1
    )
    xf = np.einsum("kabx,pq->kapqbx", xf, np.eye(2)).reshape(64, 512) * scaling
    cy = cos_y.reshape(64, 2, 16)
    sy = sin_y.reshape(64, 2, 16)
    yf = np.stack([np.stack([cy, sy], 0), np.stack([-sy, cy], 0)], 0)
    yf = np.einsum("abpyq,mn->ymaqpbn", yf, np.eye(2)).reshape(128, 256)
    xi = np.stack(
        [np.stack([cos_x.T, sin_x.T], 1), np.stack([-sin_x.T, cos_x.T], 1)], 0
    )
    xi = np.einsum("akbx,mn->maknbx", xi, np.eye(2)).reshape(64, 512) * scaling
    xi_high, xi_low = halves(xi)
    return (
        left(zf),
        left(xf),
        left(yf),
        left(yf.T.reshape(16, 4, 4, 128).swapaxes(0, 1).reshape(256, 128)),
        np.concatenate([xi_high, xi_low, xi_high], axis=0),
        left(zf.T),
    )


Z_ORDER = (0, 2, 1, 3)
RING = (0, 1, 2, 1)
FAR_FIRST = sorted(
    ((dy, dx) for dy in range(4) for dx in range(4)), key=lambda d: -RING[d[0]] - RING[d[1]]
)


def split(value):
    high = value.astype(BF16)
    return high, (value - high.astype(F32)).astype(BF16)


def rows_of(value):
    high, low = split(value)
    return jnp.concatenate([high, high, low], axis=0)


def lanes_of(value):
    high, low = split(value)
    return jnp.concatenate([high, high, low], axis=1)


def dot(a, b):
    return jnp.dot(a, b, preferred_element_type=F32)


def dot_nt(a, b):
    return lax.dot_general(a, b, (((1,), (1,)), ((), ())), preferred_element_type=F32)


def dot_tn(a, b):
    return lax.dot_general(a, b, (((0,), (0,)), ((), ())), preferred_element_type=F32)


def iota(shape, dim):
    return lax.broadcasted_iota(jnp.int32, shape, dim)


def roll(value, shift):
    shift = shift % value.shape[1]
    return value if shift == 0 else pltpu.roll(value, shift, 1)


def z_forward(r, block2, t, pair):
    res = dot(r.zf[...], rows_of(block2))
    order = (t % 2) * 2 + t // 2
    for half in range(2):
        row = order * 32 + (2 * pair + half) * 8
        for kz in range(8):
            for ri in range(2):
                k = kz * 2 + ri
                r.modes[kz // 2, pl.ds(row, 8), pl.ds(((kz % 2) * 2 + ri) * 128, 128)] = res[
                    k * 8 : k * 8 + 8, half * 128 : half * 128 + 128
                ]


def x_forward(r, send, dispatch):
    for kzp in Z_ORDER:
        res = dot_nt(r.xf[...], lanes_of(r.modes[kzp]))
        send[kzp * 16 : kzp * 16 + 16] = res.reshape(16, 4, 128)
        dispatch(kzp)


def y_forward(r, recv):
    lane = iota((16, 128), 1)
    got = recv[...].reshape(256, 128)
    res = dot(r.yf[...], rows_of(got))
    res = res[0:64] + roll(res[64:128], 64)
    rows = []
    for b in range(2):
        total = jnp.zeros((16, 128), F32)
        for g in range(4):
            piece = roll(res[g * 16 : g * 16 + 16], (g - b) * 32)
            total = jnp.where(lane // 32 == g, piece, total)
        rows.append(total)
    return jnp.concatenate(rows, axis=0)


def y_inverse(r, value, send, dispatch):
    lane = iota((16, 128), 1)
    tops = []
    for g in range(4):
        first = roll(value[0:16], -g * 32)
        second = roll(value[16:32], (1 - g) * 32)
        tops.append(jnp.where(lane < 32, first, jnp.where(lane < 64, second, 0.0)))
    top = jnp.concatenate(tops, axis=0)
    both = jnp.concatenate([top, roll(top, 64)], axis=0)
    both = rows_of(both)
    for to_z in Z_ORDER:
        res = dot(r.yi[to_z * 64 : to_z * 64 + 64, :], both)
        send[to_z * 16 : to_z * 16 + 16] = res.reshape(16, 4, 128)
        dispatch(to_z)


def masked(parts, j):
    row_q = iota((32, 128), 0) % 16
    picks = [row_q == 2 * j, row_q == 2 * j + 1]

    def pick(part):
        wide = part.astype(F32)
        return jnp.concatenate(
            [jnp.where(p, wide, 0.0).astype(BF16) for p in picks], axis=1
        )

    return pick(parts[0]), pick(parts[1])


def x_inverse(r, recv):
    r.flat[...] = recv[...].reshape(256, 128)
    for g in range(4):
        pieces = []
        for k2 in range(2):
            for ri in range(2):
                pieces.append(r.flat[pl.ds(g * 4 + ri * 2 + k2, 16, stride=16), :])
        block = rows_of(jnp.concatenate(pieces, axis=0))
        r.spread[g // 2, :, g % 2 * 512 : g % 2 * 512 + 512] = dot_tn(block, r.xi[...])


def z_inverse(r, t, pair):
    order = (t % 2) * 2 + t // 2
    columns = []
    for half in range(2):
        row = order * 32 + (2 * pair + half) * 8
        tiles = []
        for k in range(16):
            tiles.append(r.spread[k // 8, pl.ds(row, 8), pl.ds((k % 8) * 128, 128)])
        columns.append(jnp.concatenate(tiles, axis=0))
    block = jnp.concatenate(columns, axis=1)
    return dot(r.zi[...], rows_of(block))


def channel_mix(table, src, dst, shift=None):
    for t in range(4):
        for pair in range(2):
            cols = []
            for half in range(2):
                zb = 2 * pair + half
                cols.append(src[t, :, pl.ds(zb * 8, 8), :].reshape(256, 128))
            res = dot(table[...], rows_of(jnp.concatenate(cols, axis=1)))
            for half in range(2):
                zb = 2 * pair + half
                part = res[:, half * 128 : half * 128 + 128].reshape(32, 8, 128)
                if shift is not None:
                    part = part + shift[...]
                dst[t, :, pl.ds(zb * 8, 8), :] = part


def pair_of(src, t, pair):
    return jnp.concatenate(
        [src[t, pl.ds((2 * pair + half) * 8, 8)].reshape(256, 128) for half in range(2)],
        axis=1,
    )


def field_modes(r, field, t):
    for pair in range(2):
        z_forward(r, pair_of(field, t, pair), t, pair)


def same_z():
    return iota((256, 256), 0) % 8 == iota((256, 256), 1) % 8


def pointwise_tables(r):
    expand = (iota((256, 32), 0) // 8 == iota((256, 32), 1)).astype(F32).astype(BF16)
    same = same_z()
    lw_high, lw_low = split(r.lw[...])
    for i, part_of in enumerate((lw_high, lw_low, lw_high)):
        once = dot_nt(expand, part_of).astype(BF16)
        r.kron_f[:, pl.ds(i * 256, 256)] = jnp.where(same, dot_nt(once, expand), 0.0).astype(BF16)
        once = dot(expand, part_of).astype(BF16)
        r.kron_b[:, pl.ds(i * 256, 256)] = jnp.where(same, dot_nt(once, expand), 0.0).astype(BF16)


    for o in range(32):
        r.shift[o] = jnp.full((8, 128), r.bias[o], F32)


def mode_tables(r):
    zeros = jnp.zeros((32, 32), F32)
    for q in range(16):
        rows = []
        for m in range(2):
            real = r.w[pl.ds((m * 2 + 0) * 512 + q, 32, stride=16), :]
            imag = r.w[pl.ds((m * 2 + 1) * 512 + q, 32, stride=16), :]
            for ri, pieces in enumerate(((real, imag), (-imag, real))):
                pieces = list(pieces)
                both = pieces + [zeros, zeros] if m == 0 else [zeros, zeros] + pieces
                rows.append(jnp.concatenate(both, axis=1))
        block = jnp.concatenate(rows, axis=0)
        r.bw_high[q], r.bw_low[q] = split(block)
        r.bwt_high[q], r.bwt_low[q] = split(block.T)


def all_modes(value, right_high, right_low):
    parts = split(value)
    lefts = [masked(parts, j) for j in range(8)]
    high = jnp.concatenate([l[0] for l in lefts], axis=1)
    low = jnp.concatenate([l[1] for l in lefts], axis=1)
    r_high = right_high[...].reshape(2048, 128)
    r_low = right_low[...].reshape(2048, 128)
    both = dot(jnp.concatenate([high, low], axis=0), r_high)
    return both[0:32] + both[32:64] + dot(high, r_low)


def mix(r, own, dispatch):
    spectrum = y_forward(r, r.recv0)
    r.s_all[own, :] = spectrum
    mixed = all_modes(spectrum, r.bw_high, r.bw_low)
    y_inverse(r, mixed, r.send1, dispatch)


def mix_adjoint(r, own, dispatch, column_sums):
    grad_modes = y_forward(r, r.recv2)
    r.g_all[own, :] = grad_modes
    column_sums()
    back = all_modes(grad_modes, r.bwt_high, r.bwt_low)
    y_inverse(r, back, r.send3, dispatch)


def cells(r, t):
    for pair in range(2):
        field = z_inverse(r, t, pair)
        for half in range(2):
            for o8 in range(8):
                o = (2 * pair + half) * 8 + o8
                pre = field[o8 * 32 : o8 * 32 + 32, half * 128 : half * 128 + 128] + r.loc[t, o]
                square = pre * pre
                bent = jnp.tanh(pre * (gelu_scale + (gelu_scale * cubic_term) * square))
                half_up = 0.5 + 0.5 * bent
                r.lay[t, o] = pre * half_up
                rise = (0.5 * gelu_scale) + (1.5 * gelu_scale * cubic_term) * square
                slope = half_up + (pre * rise) * (1.0 - bent * bent)
                grad = r.cot[t, o] * slope
                r.gp[t, o] = grad


def point_sums(r):
    same = same_z()
    for t in range(4):
        a_cols = [r.v[t, :, pl.ds(zb * 8, 8), :].reshape(256, 128) for zb in range(4)]
        b_cols = [r.gp[t, :, pl.ds(zb * 8, 8), :].reshape(256, 128) for zb in range(4)]
        a_high, a_low = split(jnp.concatenate(a_cols, axis=1))
        b_high, b_low = split(jnp.concatenate(b_cols, axis=1))
        term = dot_nt(
            jnp.concatenate([a_high, a_high, a_low], axis=1),
            jnp.concatenate([b_high, b_low, b_high], axis=1),
        )
        r.acc[...] = term if t == 0 else r.acc[...] + term
    folded = jnp.sum(jnp.where(same, r.acc[...], 0.0).reshape(32, 8, 256), axis=1)
    pick = (iota((256, 128), 0) // 8 == iota((256, 128), 1)).astype(F32).astype(BF16)
    fold_high, fold_low = split(folded)
    pointwise = dot(
        jnp.concatenate([fold_high, fold_low], axis=1), jnp.concatenate([pick, pick], axis=0)
    )
    dense = pointwise[0:8]
    for k in range(1, 4):
        dense = dense + roll(pointwise[8 * k : 8 * k + 8], 32 * k)
    sums = jnp.sum(r.gp[0], axis=1)
    for t in range(1, 4):
        sums = sums + jnp.sum(r.gp[t], axis=1)
    sum_high, sum_low = split(sums)
    ones = jnp.ones((8, 256), BF16)
    bias_row = dot_nt(
        ones,
        jnp.concatenate(
            [jnp.concatenate([sum_high, sum_low], axis=1), jnp.zeros((96, 256), BF16)], axis=0
        ),
    )
    for i in range(8):
        r.part1[i] = dense[i : i + 1]
    r.part1[8] = bias_row[0:1]


def weight_gradient(r):
    lane8 = iota((8, 128), 1)
    sign = jnp.where(lane8 // 32 % 2 == 0, 1.0, -1.0)
    low_half = lane8 < 64
    for q in range(16):
        s_q = r.s_all[pl.ds(q, 8, stride=16), :]
        g_q = r.g_all[pl.ds(q, 8, stride=16), :]
        first = s_q * sign
        second = jnp.where(lane8 // 32 % 2 == 0, roll(s_q, -32), roll(s_q, 32))
        left_rows = jnp.concatenate(
            [
                jnp.where(low_half, first, 0.0),
                jnp.where(low_half, second, 0.0),
                jnp.where(low_half, 0.0, first),
                jnp.where(low_half, 0.0, second),
            ],
            axis=0,
        )
        right_rows = jnp.concatenate([roll(g_q, -32 * g) for g in range(4)], axis=0)
        l_high, l_low = split(left_rows)
        r_high, r_low = split(right_rows)
        res = dot_tn(
            jnp.concatenate([l_high, l_high, l_low], axis=0),
            jnp.concatenate([r_high, r_low, r_high], axis=0),
        )
        r.gspec[pl.ds(q, 128, stride=16), :] = res[:, 0:32]


def final_cells(r, t):
    for pair in range(2):
        field = z_inverse(r, t, pair)
        for half in range(2):
            ob = 2 * pair + half
            r.res[t, pl.ds(ob * 8, 8)] = r.loc[t, pl.ds(ob * 8, 8)] + field[
                :, half * 128 : half * 128 + 128
            ].reshape(8, 32, 128)


CELLS, SLOTS = (4, 32, 32, 128), (64, 4, 128)
IN_NAMES = ["v", "w", "lw", "bias", "cot", "zf", "xf", "yf", "yi", "xi", "zi"]
OUT_SHAPES = dict(
    lay=(CELLS, F32), loc=(CELLS, F32), s_all=((128, 128), F32), g_all=((128, 128), F32), recv3=(SLOTS, F32),
    total=((16, 9, 1, 128), F32), xi=((192, 512), BF16), zi=((256, 384), BF16),
)
SCRATCH = dict(
    v=(CELLS, F32), w=((2048, 32), F32), lw=((32, 32), F32), cot=(CELLS, F32),
    zf=((128, 768), BF16), xf=((64, 1536), BF16), yf=((128, 768), BF16), yi=((256, 384), BF16),
    modes=((4, 128, 512), F32), gp=(CELLS, F32),
    bw_high=((16, 128, 128), BF16), bw_low=((16, 128, 128), BF16),
    bwt_high=((16, 128, 128), BF16), bwt_low=((16, 128, 128), BF16),
    kron_f=((256, 768), BF16), kron_b=((256, 768), BF16),
    flat=((256, 128), F32), spread=((2, 128, 1024), F32),
    acc=((256, 256), F32),
    part1=((9, 1, 128), F32), stage1=((16, 9, 1, 128), F32), part2=((9, 1, 128), F32),
    shift=((32, 8, 128), F32),
    send0=(SLOTS, F32), send1=(SLOTS, F32), send2=(SLOTS, F32), send3=(SLOTS, F32),
    recv0=(SLOTS, F32), recv1=(SLOTS, F32), recv2=(SLOTS, F32),
)
SEMAPHORES = dict(in_sem=16, send_sem=6, recv_sem=6, small_send=2, small_recv=2)


def kernel(*refs):
    names = [n + "_hbm" for n in IN_NAMES]
    names += list(OUT_SHAPES) + list(SCRATCH) + ["bias"] + list(SEMAPHORES)
    r = types.SimpleNamespace(**dict(zip(names, refs, strict=True)))
    me = lax.axis_index("pencil")
    group = lax.axis_index("batch")
    my_y, my_x, my_z = me // 16, me // 4 % 4, me % 4
    across = (group + 2) % GROUPS

    def peer_of(dy, dx, to_z):
        return (my_y + dy) % 4 * 16 + (my_x + dx) % 4 * 4 + to_z

    barrier = pltpu.get_barrier_semaphore()
    for dy, dx in FAR_FIRST:
        for to_z in range(4):
            pl.semaphore_signal(
                barrier, inc=1, device_id=(across, peer_of(dy, dx, to_z)), device_id_type=MESH
            )
    greetings = PEERS
    around = []
    for dg in range(4):
        for dz in range(4):
            if dg == 0 and dz == 0:
                continue
            near = ((group + dg) % GROUPS, me - my_z + (my_z + dz) % 4)
            around.append(near)
            if dg != 2:
                greetings += 1
                pl.semaphore_signal(barrier, inc=1, device_id=near, device_id_type=MESH)

    for dy, dx in FAR_FIRST[:-1]:
        greetings += 1
        pl.semaphore_signal(
            barrier, inc=1, device_id=(group, peer_of(dy, dx, my_z)), device_id_type=MESH
        )

    loads = {}

    def load(name, src, dst):
        loads[name] = pltpu.make_async_copy(src, dst, r.in_sem.at[len(loads)])
        loads[name].start()

    load("zf", r.zf_hbm, r.zf)
    for t in range(4):
        load("v%d" % t, r.v_hbm.at[t], r.v.at[t])
    for name in ("xf", "bias", "lw", "w", "yf", "yi", "xi", "zi", "cot"):
        load(name, getattr(r, name + "_hbm"), getattr(r, name))

    def send_to(send, recv, index):
        def dispatch(to_z):
            for dy, dx in FAR_FIRST:
                peer = peer_of(dy, dx, to_z)
                pltpu.make_async_remote_copy(
                    src_ref=send.at[to_z * 16 + peer // 4],
                    dst_ref=recv.at[me],
                    send_sem=r.send_sem.at[index],
                    recv_sem=r.recv_sem.at[index],
                    device_id=(across, peer),
                    device_id_type=MESH,
                ).start()

        return dispatch

    def await_bytes(ref, sem):
        pltpu.make_async_copy(ref, ref, sem).wait()

    own = pl.ds(pl.multiple_of(group * 32, 32), 32)

    def share(buffer, index):
        for dg in (2, 1, 3):
            pltpu.make_async_remote_copy(
                src_ref=buffer.at[own],
                dst_ref=buffer.at[own],
                send_sem=r.send_sem.at[index],
                recv_sem=r.recv_sem.at[index],
                device_id=((group + dg) % GROUPS, me),
                device_id_type=MESH,
            ).start()

    spot = group * 4 + my_z
    fifteen = pl.ds(0, 15)

    loads["zf"].wait()
    for t in range(4):
        loads["v%d" % t].wait()
        field_modes(r, r.v, t)
    loads["xf"].wait()
    x_forward(r, r.send0, lambda to_z: None)
    pl.semaphore_wait(barrier, greetings)
    for to_z in Z_ORDER:
        send_to(r.send0, r.recv0, 0)(to_z)

    loads["lw"].wait()
    loads["bias"].wait()
    pointwise_tables(r)
    loads["w"].wait()
    mode_tables(r)
    channel_mix(r.kron_f, r.v, r.loc, r.shift)

    loads["yf"].wait()
    loads["yi"].wait()
    await_bytes(r.recv0, r.recv_sem.at[0])
    mix(r, own, send_to(r.send1, r.recv1, 1))

    loads["xi"].wait()
    loads["zi"].wait()
    loads["cot"].wait()
    await_bytes(r.recv1, r.recv_sem.at[1])
    share(r.s_all, 4)
    x_inverse(r, r.recv1)
    for t in range(4):
        cells(r, t)
    for t in range(4):
        field_modes(r, r.gp, t)
    x_forward(r, r.send2, send_to(r.send2, r.recv2, 2))

    point_sums(r)
    for dy, dx in FAR_FIRST[:-1]:
        pltpu.make_async_remote_copy(
            src_ref=r.part1,
            dst_ref=r.stage1.at[me // 4],
            send_sem=r.small_send.at[0],
            recv_sem=r.small_recv.at[0],
            device_id=(group, peer_of(dy, dx, my_z)),
            device_id_type=MESH,
        ).start()
    r.stage1[me // 4] = r.part1[...]
    channel_mix(r.kron_b, r.gp, r.loc)

    await_bytes(r.recv2, r.recv_sem.at[2])

    def column_sums():
        await_bytes(r.stage1.at[fifteen], r.small_recv.at[0])
        r.part2[...] = jnp.sum(r.stage1[...], axis=0)
        for to_group, to_peer in around:
            pltpu.make_async_remote_copy(
                src_ref=r.part2,
                dst_ref=r.total.at[spot],
                send_sem=r.small_send.at[1],
                recv_sem=r.small_recv.at[1],
                device_id=(to_group, to_peer),
                device_id_type=MESH,
            ).start()
        r.total[spot] = r.part2[...]

    mix_adjoint(r, own, send_to(r.send3, r.recv3, 3), column_sums)
    share(r.g_all, 5)

    for buffer, index in ((r.s_all, 4), (r.g_all, 5)):
        await_bytes(buffer.at[pl.ds(0, 96)], r.recv_sem.at[index])

    for index, buffer in enumerate((r.send0, r.send1, r.send2, r.send3)):
        await_bytes(buffer, r.send_sem.at[index])
    for index, buffer in ((4, r.s_all), (5, r.g_all)):
        await_bytes(buffer.at[pl.ds(0, 96)], r.send_sem.at[index])
    await_bytes(r.stage1.at[fifteen], r.small_send.at[0])
    await_bytes(r.total.at[fifteen], r.small_send.at[1])
    await_bytes(r.total.at[fifteen], r.small_recv.at[1])
    await_bytes(r.recv3, r.recv_sem.at[3])


TAIL_SCRATCH = dict(
    flat=((256, 128), F32), spread=((2, 128, 1024), F32), res=(CELLS, F32), gspec=((2048, 32), F32),
)


def tail(*refs):
    names = list(OUT_SHAPES) + ["layer_out", "grad_state", "grad_spectral", "grad_local", "grad_bias"]
    names += list(TAIL_SCRATCH) + ["sem"]
    r = types.SimpleNamespace(**dict(zip(names, refs, strict=True)))
    copies = []

    def copy(src, dst):
        copies.append(pltpu.make_async_copy(src, dst, r.sem.at[len(copies)]))
        copies[-1].start()

    copy(r.lay, r.layer_out)
    weight_gradient(r)
    copy(r.gspec, r.grad_spectral)
    total = jnp.sum(r.total[...], axis=0).reshape(9, 128) * (1.0 / math.sqrt(8 * X * Y * Z))
    for k in range(4):
        r.grad_local[pl.ds(8 * k, 8), :] = roll(total[0:8], -32 * k)[:, 0:32]
    r.grad_bias[...] = total[8:9, 0:32]
    x_inverse(r, r.recv3)
    for t in range(4):
        final_cells(r, t)
        copy(r.res.at[t], r.grad_state.at[t])
    for pending in copies:
        pending.wait()


def vmem(array):
    return pltpu.with_memory_space_constraint(array, pltpu.VMEM)


def hbm(array):
    return pltpu.with_memory_space_constraint(array, pltpu.HBM)


def shards(state_field, spectral_weight, local_weight, channel_bias, cotangent):
    tables = [hbm(jnp.asarray(t)) for t in build_tables()]
    in_hbm = pl.BlockSpec(memory_space=pltpu.HBM)
    in_vmem = pl.BlockSpec(memory_space=pltpu.VMEM)
    held = pl.pallas_call(
        kernel,
        out_shape=tuple(pltpu.VMEM(*s) for s in OUT_SHAPES.values()),
        in_specs=[in_hbm] * len(IN_NAMES),
        out_specs=(in_vmem,) * len(OUT_SHAPES),
        scratch_shapes=[pltpu.VMEM(*s) for s in SCRATCH.values()]
        + [pltpu.SMEM((32,), F32)]
        + [pltpu.SemaphoreType.DMA((n,)) for n in SEMAPHORES.values()],
        compiler_params=pltpu.CompilerParams(
            collective_id=0, has_side_effects=True, vmem_limit_bytes=40 * 1024 * 1024
        ),
        name="fno_layer",
    )(
        hbm(state_field.reshape(CELLS)),
        hbm(jnp.swapaxes(spectral_weight, 3, 4).reshape(2048, 32)),
        hbm(local_weight),
        hbm(channel_bias),
        hbm(cotangent.reshape(CELLS)),
        *tables,
    )
    out = pl.pallas_call(
        tail,
        out_shape=(
            jax.ShapeDtypeStruct(CELLS, F32),
            jax.ShapeDtypeStruct(CELLS, F32),
            jax.ShapeDtypeStruct((2048, 32), F32),
            jax.ShapeDtypeStruct((32, 32), F32),
            jax.ShapeDtypeStruct((1, 32), F32),
        ),
        in_specs=[in_vmem] * len(OUT_SHAPES),
        out_specs=(in_hbm, in_hbm, in_hbm, in_vmem, in_vmem),
        scratch_shapes=[pltpu.VMEM(*s) for s in TAIL_SCRATCH.values()]
        + [pltpu.SemaphoreType.DMA((6,))],
        compiler_params=pltpu.CompilerParams(vmem_limit_bytes=24 * 1024 * 1024),
        name="fno_tail",
    )(*[vmem(h) for h in held])
    layer_out, grad_state, grad_spectral, grad_local, grad_bias = out
    return (
        layer_out.reshape(state_field.shape),
        grad_state.reshape(state_field.shape),
        jnp.swapaxes(grad_spectral.reshape(2, 2, 32, 16, 32), 3, 4),
        grad_local,
        grad_bias.reshape(32),
    )


def solution(mesh):
    cells = P("batch", "pencil", None, None, None)
    modes = P("pencil", None, None, None, None)
    return jax.shard_map(
        shards,
        mesh=mesh,
        in_specs=(cells, modes, P(), P(), cells),
        out_specs=(cells, cells, modes, P(), P()),
        check_vma=False,
    )
```
